128 devices in a mesh: grp: 2 (over z_hi), ctx: 16 (over x, y), head: 4 (over z_lo, core).
Axes of the slice: x: 4, y: 4, z: 4 (z_hi: 2, z_lo: 2; z = z_hi * 2 + z_lo), core: 2. Of those that a mesh axis runs over, the one named last changes fastest.
Arguments:
- queries: bfloat16 [4, 2048, 5120], P('grp', 'ctx', 'head'), may hold values from -32 to 32
- keys: bfloat16 [4, 2048, 1024], P('grp', 'ctx', 'head'), may hold values from -6 to 6
- values: bfloat16 [4, 2048, 1024], P('grp', 'ctx', 'head'), may hold values from -6 to 6
- prefix_keys: bfloat16 [4096, 1024], P(('grp', 'ctx'), 'head'), may hold values from -16 to 16
- shared_prompt_values: bfloat16 [4096, 1024], P(('grp', 'ctx'), 'head'), may hold values from -6 to 6
- lengths: int32 [4], P('grp'), may hold values from 512 to 2048, as said below
- grad_out: bfloat16 [4, 2048, 5120], P('grp', 'ctx', 'head'), may hold values from -6 to 6
Outputs:
- attended: bfloat16 [4, 2048, 5120], P('grp', 'ctx', 'head')
- query_grad: bfloat16 [4, 2048, 5120], P('grp', 'ctx', 'head')
- key_grad: bfloat16 [4, 2048, 1024], P('grp', 'ctx', 'head')
- value_grad: bfloat16 [4, 2048, 1024], P('grp', 'ctx', 'head')
- prefix_key_grad: bfloat16 [4096, 1024], P(('grp', 'ctx'), 'head')
- prefix_value_grad: bfloat16 [4096, 1024], P(('grp', 'ctx'), 'head')
The draws below stay inside these ranges and needn't reach their ends.
Inputs may be any that keep to these rules, and one draw needn't show every extreme that they name: `lengths`: one response has exactly 2048 live positions and another exactly 512.
All inputs are finite; a program needn't handle non-finite values.
Results may differ from the reference program's by a relative error of at most 0.04.
Values may be sent and summed in bfloat16 or wider, within the bound.
A program may use at most 192 MiB of HBM per device.

```python
import math
import jax
import jax.numpy as jnp
from jax import lax

QUERY_HEADS = 40
KEY_VALUE_HEADS = 8
HEAD_SIZE = 128
RESPONSE_LENGTH = 2048
PREFIX_TOKENS = 4096
RESPONSE_COUNT = 4


def draw_prefix_keys(key, part):
    key = jax.random.fold_in(key, 11)
    base_offset = jnp.clip(jax.random.normal(key, (PREFIX_TOKENS, KEY_VALUE_HEADS * HEAD_SIZE), jnp.float32), -5.0, 5.0)
    return base_offset.astype(jnp.bfloat16)


def draw_queries(key, part):
    key = jax.random.fold_in(key, 12)
    base_offset = jnp.clip(jax.random.normal(key, (RESPONSE_COUNT, RESPONSE_LENGTH, QUERY_HEADS * HEAD_SIZE), jnp.float32), -5.0, 5.0)
    return base_offset.astype(jnp.bfloat16)


def draw_lengths(key, part):
    key = jax.random.fold_in(key, 13)
    order = jax.random.permutation(key, RESPONSE_COUNT)
    drawn = jax.random.randint(jax.random.fold_in(key, 1), (RESPONSE_COUNT,), RESPONSE_LENGTH // 4, RESPONSE_LENGTH + 1, jnp.int32)
    drawn = drawn.at[order[0]].set(RESPONSE_LENGTH)
    drawn = drawn.at[order[1]].set(RESPONSE_LENGTH // 4)
    return drawn.astype(jnp.int32)


def levels(rng, extent, pieces, low, high):
    def one(dim, parts):
        draws = jax.random.uniform(jax.random.fold_in(jax.random.fold_in(rng, 6), dim), (parts,), jnp.float32, low / len(pieces), high / len(pieces))
        return jnp.repeat(jnp.exp(draws), extent[dim] // parts).reshape((-1,) + (1,) * (len(extent) - dim - 1))

    gain = one(*pieces[0])
    for cut in pieces[1:]:
        gain = gain * one(*cut)
    return gain


def normal_values(rng, extent, width, bound, pieces=(), held_as=jnp.bfloat16):
    result = jax.random.normal(rng, extent, jnp.float32) * width
    if len(pieces) > 0:
        result = levels(rng, extent, pieces, -0.22, 0.18) * result
    return jnp.clip(result, min=-bound, max=bound).astype(held_as)


def setup_inputs(seed: int = 0) -> dict:
    arg_keys = jax.random.split(jax.random.key(seed), 8)
    queries = draw_queries(jax.random.fold_in(arg_keys[7], 71), 0)
    keys = normal_values(arg_keys[1], (RESPONSE_COUNT, RESPONSE_LENGTH, KEY_VALUE_HEADS * HEAD_SIZE), 1.0, 6.0, ((0, 2), (1, 16), (2, 4)))
    values = normal_values(arg_keys[2], (RESPONSE_COUNT, RESPONSE_LENGTH, KEY_VALUE_HEADS * HEAD_SIZE), 1.0, 6.0, ((0, 2), (1, 16), (2, 4)))
    prefix_keys = draw_prefix_keys(jax.random.fold_in(arg_keys[7], 71), 0)
    shared_prompt_values = normal_values(arg_keys[4], (PREFIX_TOKENS, KEY_VALUE_HEADS * HEAD_SIZE), 1.0, 6.0, ((0, 32), (1, 4)))
    lengths = draw_lengths(jax.random.fold_in(arg_keys[7], 71), 0)
    grad_out = normal_values(arg_keys[6], (RESPONSE_COUNT, RESPONSE_LENGTH, QUERY_HEADS * HEAD_SIZE), 1.0, 6.0, ((0, 2), (1, 16), (2, 4)))
    return dict(queries=queries, keys=keys, values=values, prefix_keys=prefix_keys, shared_prompt_values=shared_prompt_values, lengths=lengths, grad_out=grad_out)


def low(x):
    return lax.optimization_barrier(x.astype(jnp.bfloat16)).astype(jnp.float32)

def one_response(query, key_row_block, value_row_block, grad, prompt_keys, prompt_values, length):
    count = query.shape[0]
    pcount = prompt_keys.shape[0]
    unique_count = pcount + count
    head_groups = QUERY_HEADS // KEY_VALUE_HEADS
    scale = 1.0 / math.sqrt(HEAD_SIZE)
    joined_keys = jnp.concatenate([prompt_keys, key_row_block], 0).astype(jnp.float32).reshape(unique_count, KEY_VALUE_HEADS, HEAD_SIZE)
    joined_values = jnp.concatenate([prompt_values, value_row_block], 0).astype(jnp.float32).reshape(unique_count, KEY_VALUE_HEADS, HEAD_SIZE)
    tpos = jnp.arange(count, dtype=jnp.int32)
    upos = jnp.arange(unique_count, dtype=jnp.int32) - pcount
    valid = tpos < length
    mask = (upos[None, :] < 0) | (upos[None, :] <= tpos[:, None]) & (upos[None, :] < length)
    glive = jnp.where(valid[:, None], grad, jnp.zeros_like(grad))
    qheads = jnp.transpose(query.astype(jnp.float32).reshape(count, QUERY_HEADS, HEAD_SIZE), (1, 0, 2))
    gheads = jnp.transpose(glive.astype(jnp.float32).reshape(count, QUERY_HEADS, HEAD_SIZE), (1, 0, 2))
    kvindex = jnp.arange(QUERY_HEADS, dtype=jnp.int32) // head_groups

    def step(carry, xs):
        key_gradient, value_gradient = carry
        qhead, ghead, kvh = xs
        khead = lax.dynamic_index_in_dim(joined_keys, kvh, 1, keepdims=False)
        vhead = lax.dynamic_index_in_dim(joined_values, kvh, 1, keepdims=False)
        scores = jnp.einsum('td,ud->tu', qhead, khead) * scale
        scores = jnp.where(mask, scores, -jnp.inf)
        top = lax.optimization_barrier(jnp.max(scores, -1, keepdims=True))
        lse = top + jnp.log(lax.optimization_barrier(jnp.sum(jnp.exp(scores - top), -1, keepdims=True)))
        probs = jnp.exp(scores - lse)
        plow = low(probs)
        outrow = jnp.einsum('tu,ud->td', plow, vhead)
        outlow = low(jnp.where(valid[:, None], outrow, 0.0))
        delta = lax.optimization_barrier(jnp.sum(ghead * outlow, -1))
        dprobs = jnp.einsum('td,ud->tu', ghead, vhead)
        dscores = low(probs * (dprobs - delta[:, None]) * scale)
        dquery = jnp.einsum('tu,ud->td', dscores, khead)
        key_gradient = key_gradient.at[:, kvh].add(jnp.einsum('tu,td->ud', dscores, qhead))
        value_gradient = value_gradient.at[:, kvh].add(jnp.einsum('tu,td->ud', plow, ghead))
        return ((key_gradient, value_gradient), (outlow, dquery))
    zero_fill = jnp.zeros((unique_count, KEY_VALUE_HEADS, HEAD_SIZE), jnp.float32)
    (key_gradient, value_gradient), (outs, dqs) = lax.scan(step, (zero_fill, zero_fill), (qheads, gheads, kvindex))
    attended = jnp.transpose(outs, (1, 0, 2)).reshape(count, QUERY_HEADS * HEAD_SIZE).astype(jnp.bfloat16)
    qgrad = jnp.transpose(dqs, (1, 0, 2)).reshape(count, QUERY_HEADS * HEAD_SIZE).astype(jnp.bfloat16)
    key_gradient = key_gradient.reshape(unique_count, KEY_VALUE_HEADS * HEAD_SIZE)
    value_gradient = value_gradient.reshape(unique_count, KEY_VALUE_HEADS * HEAD_SIZE)
    return (attended, qgrad, key_gradient[pcount:], value_gradient[pcount:], key_gradient[:pcount], value_gradient[:pcount])

def reference(queries, keys, values, prefix_keys, shared_prompt_values, lengths, grad_out):
    outs, qgrads, kgrads, vgrads = ([], [], [], [])
    pk_total = jnp.zeros(prefix_keys.shape, jnp.float32)
    pv_total = jnp.zeros(prefix_keys.shape, jnp.float32)
    for index in range(queries.shape[0]):
        res = one_response(queries[index], keys[index], values[index], grad_out[index], prefix_keys, shared_prompt_values, lengths[index])
        outs.append(res[0])
        qgrads.append(res[1])
        kgrads.append(res[2].astype(jnp.bfloat16))
        vgrads.append(res[3].astype(jnp.bfloat16))
        pk_total = pk_total + res[4]
        pv_total = pv_total + res[5]
    return (jnp.stack(outs), jnp.stack(qgrads), jnp.stack(kgrads), jnp.stack(vgrads), pk_total.astype(jnp.bfloat16), pv_total.astype(jnp.bfloat16))
```

```python
import functools
import math

import jax
import jax.numpy as jnp
from jax import lax
from jax.experimental import pallas as pl
from jax.experimental.pallas import tpu as pltpu
from jax.sharding import PartitionSpec as P

MESH = pl.DeviceIdType.MESH
F32, BF = jnp.float32, jnp.bfloat16
T = 128
CH = 512
HEADS = 5
R = HEADS * T
PC = 8
NT = (((1,), (1,)), ((), ()))
NN = (((1,), (0,)), ((), ()))
dot = functools.partial(lax.dot_general, preferred_element_type=F32)
N_SEM = 64


def mult(v, n):
    return pl.multiple_of(v, n)


def kernel(
    lens_ref, queries, keys, values, pkeys, pvalues, gout,
    attended, query_grad, key_grad, value_grad, pk_grad, pv_grad,
    q_ref, g_ref, kv, rbuf, pbuf, o_ref, dq_ref,
    ka, va, qa, ga, gt, gs, s_ref, e_ref, mrun, stat, turned, top_ref, acc,
    send, recv, lsem,
):
    grp, ctx, head = lax.axis_index("grp"), lax.axis_index("ctx"), lax.axis_index("head")
    x, y = ctx // 4, ctx % 4
    resp, kvh = x // 2, x % 2
    c2 = 1.4426950408889634 / math.sqrt(T)
    scale = 1.0 / math.sqrt(T)

    def xdev(d, other=0):
        return ((grp + other) % 2, ((x + d) % 4) * 4 + y, head)

    def ydev(d):
        return (grp, x * 4 + (y + d) % 4, head)

    counter = [0, 0]

    def remote(src, dst, dev):
        k = counter[0]
        counter[0] += 1
        return pltpu.make_async_remote_copy(
            src_ref=src, dst_ref=dst, send_sem=send.at[k], recv_sem=recv.at[k],
            device_id=dev, device_id_type=MESH,
        )

    def local(src, dst):
        k = counter[1]
        counter[1] += 1
        return pltpu.make_async_copy(src, dst, lsem.at[k])

    partners = [xdev(d) for d in (1, 2, 3)] + [ydev(d) for d in (1, 2, 3)] + [xdev(d, 1) for d in range(4)]
    barrier = pltpu.get_barrier_semaphore()
    for dev in partners:
        pl.semaphore_signal(barrier, inc=1, device_id=dev, device_id_type=MESH)
    pl.semaphore_wait(barrier, len(partners))

    def hd(j):
        return pl.ds(mult(j * T, T), T)

    def wide(j):
        return pl.ds(mult(j * R, T), R)

    def blk(b):
        return pl.ds(mult(b * T, T), T)

    pre, late = [], []
    for other in (1, 0):
        for d in range(4):
            tx = (x + d) % 4
            j = tx % 2
            copy = local if (d == 0 and not other) else functools.partial(remote, dev=xdev(d, other))
            for which, ref in ((0, pkeys), (1, pvalues)):
                pre.append(copy(ref.at[:, hd(j)], kv.at[y, which, blk(grp * 4 + x), :]))
    for d in range(4):
        tx = (x + d) % 4
        r, j = tx // 2, tx % 2
        copy = local if d == 0 else functools.partial(remote, dev=xdev(d))
        for which, ref in ((0, keys), (1, values)):
            pre.append(copy(ref.at[r, :, hd(j)], kv.at[y, which, blk(8 + x), :]))
        for ref, buf in ((queries, q_ref), (gout, g_ref)):
            late.append(copy(ref.at[r, :, wide(j)], buf.at[x]))
    for copy in pre + late:
        copy.start()
    for copy in pre:
        copy.wait()

    ygather = {}
    for d in (2, 1, 3):
        ygather[d] = [
            remote(kv.at[y, :, pl.ds(0, 1024), :], kv.at[y, :, pl.ds(0, 1024), :], ydev(d)),
            remote(kv.at[y, :, pl.ds(1024, 512), :], kv.at[y, :, pl.ds(1024, 512), :], ydev(d)),
        ]
        for copy in ygather[d]:
            copy.start()
    for copy in late:
        copy.wait()

    def place(d):
        sy = (y - d) % 4
        ps = pl.ds(d * 1024, 1024)
        ka[ps, :T] = kv[sy, 0, :1024, :]
        ka[ps, T:] = kv[sy, 0, :1024, :]
        va[ps, :T] = kv[sy, 1, :1024, :]
        va[ps, T:] = jnp.ones((1024, T), BF)
        for i in range(4):
            rs = pl.ds(mult(4096 + i * CH + sy * T, T), T)
            src = slice(1024 + i * T, 1024 + (i + 1) * T)
            ka[rs, :T] = kv[sy, 0, src, :]
            ka[rs, T:] = kv[sy, 0, src, :]
            va[rs, :T] = kv[sy, 1, src, :]
            va[rs, T:] = jnp.ones((T, T), BF)

    def off(i):
        return PC * i + (i * (i + 1)) // 2

    def chunk_rows(c):
        return pl.ds(mult(c * CH, CH), CH)

    def fold(s):
        return functools.reduce(jnp.maximum, [s[:, k * T:(k + 1) * T] for k in range(CH // T)])

    lane = lax.broadcasted_iota(jnp.int32, (R, T), 1)

    def prepare(i, _):
        for h in range(HEADS):
            rs = slice(h * T, (h + 1) * T)
            qs = q_ref[i, :, rs].astype(F32) * c2
            hi = qs.astype(BF)
            qa[i, rs, :T] = hi
            qa[i, rs, T:] = (qs - hi.astype(F32)).astype(BF)
        acc[i] = jnp.zeros((R, 2 * T), F32)
        mrun[i] = jnp.full((R, T), -jnp.inf, F32)
        stat[i] = jnp.zeros((R, T), F32)
        return 0

    lax.fori_loop(0, 4, prepare, 0)

    def scores(i, c, slot):
        s = dot(qa[i], ka[chunk_rows(c), :], NT)
        s_ref[slot] = s
        return fold(s)

    def weigh(i, base, count, g, top):
        old = mrun[i]
        new = jnp.maximum(old, jnp.broadcast_to(jnp.max(top, 1, keepdims=True), (R, T)))
        mrun[i] = new
        stat[i] = jnp.where(lane == g, new, stat[i])
        fade = jnp.exp2(old - new)
        acc[i, :, :T] *= fade
        acc[i, :, T:] *= fade

        def exps(n, _):
            c = base + n
            mm = mrun[i]
            s = s_ref[n]
            e = jnp.concatenate(
                [jnp.exp2(s[:, k * T:(k + 1) * T] - mm) for k in range(CH // T)], 1
            ).astype(BF)
            e_ref[off(i) + c] = e
            acc[i] += dot(e, va[chunk_rows(c), :], NN)
            return 0

        lax.fori_loop(0, count, exps, 0)

    def prefix_group(d, g):
        def tile(i, _):
            top = jnp.maximum(scores(i, 2 * d, 0), scores(i, 2 * d + 1, 1))
            weigh(i, 2 * d, 2, g, top)
            return 0

        lax.fori_loop(0, 4, tile, 0)

    def response_tile(i, _):
        top_ref[...] = jnp.full((R, T), -jnp.inf, F32)

        def one(n, _):
            top_ref[...] = jnp.maximum(top_ref[...], scores(i, PC + n, n))
            return 0

        lax.fori_loop(0, i, one, 0)
        s = dot(qa[i], ka[chunk_rows(PC + i), :], NT)
        col = lax.broadcasted_iota(jnp.int32, (T, CH), 1)
        row = lax.broadcasted_iota(jnp.int32, (T, CH), 0) + y * T
        seen = col <= row
        s = jnp.concatenate(
            [jnp.where(seen, s[h * T:(h + 1) * T], -jnp.inf) for h in range(HEADS)], 0
        )
        s_ref[i] = s
        weigh(i, PC, i + 1, 4, jnp.maximum(top_ref[...], fold(s)))
        stat[i] = jnp.exp2(stat[i] - mrun[i])
        pos = lax.broadcasted_iota(jnp.int32, (T, T), 0) + (i * CH + y * T)
        live = pos < lens_ref[resp]
        part = lax.broadcasted_iota(jnp.int32, (T, T), 1)
        for h in range(HEADS):
            rs = slice(h * T, (h + 1) * T)
            inv = 1.0 / acc[i, rs, T:]
            o = jnp.where(live, acc[i, rs, :T] * inv, 0.0).astype(BF)
            o_ref[i, :, rs] = o
            g = jnp.where(live, g_ref[i, :, rs].astype(F32), 0.0)
            d0 = -jnp.sum(g * o.astype(F32), 1, keepdims=True)
            d1 = d0.astype(BF).astype(F32)
            d2 = (d0 - d1).astype(BF).astype(F32)
            d3 = d0 - d1 - d2
            ga[i, rs, :T] = g.astype(BF)
            ga[i, rs, T:] = jnp.where(
                part == 0, d1, jnp.where(part == 1, d2, jnp.where(part == 2, d3, 0.0))
            ).astype(BF)
            gt[0, i, :, rs] = (q_ref[i, :, rs].astype(F32) * (inv * scale)).astype(BF).T
            gt[1, i, :, rs] = (g * inv).astype(BF).T
            turned[i, :, rs] = stat[i, rs, :].T[:8]
            acc[i, rs, T:] = inv * scale
        acc[i, :, :T] = jnp.zeros((R, T), F32)
        return 0

    order = (0, 2, 1, 3)
    place(0)
    prefix_group(0, 0)
    for g in (1, 2, 3):
        for copy in ygather[order[g]]:
            copy.wait()
        place(order[g])
        prefix_group(order[g], g)
    lax.fori_loop(0, 4, response_tile, 0)

    homes = []
    for d in range(4):
        tx = (x + d) % 4
        copy = local if d == 0 else functools.partial(remote, dev=xdev(d))
        homes.append(copy(o_ref.at[tx], attended.at[resp, :, wide(kvh)]))
    for copy in homes:
        copy.start()

    def scaled(g):
        def turn(i, _):
            f = turned[i, g:g + 1, :]
            for w in range(2):
                gs[w, i] = (gt[w, i].astype(F32) * f).astype(BF)
            return 0

        lax.fori_loop(0, 4, turn, 0)

    def grads(c, first, g):
        kk = chunk_rows(c)
        s_ref[0, :2 * T, :] = jnp.zeros((2 * T, CH), F32)

        def row(i, _):
            e = e_ref[off(i) + c]
            dp = dot(ga[i], va[kk, :], NT)
            ds = (e.astype(F32) * dp).astype(BF)
            acc[i, :, :T] += stat[i, :, g:g + 1] * dot(ds, ka[kk, :T], NN)
            s_ref[0, :T, :] += dot(gs[0, i], ds, NN)
            s_ref[0, T:2 * T, :] += dot(gs[1, i], e, NN)
            return 0

        lax.fori_loop(first, 4, row, 0)
        return [s_ref[0, w * T:(w + 1) * T, :].T.astype(BF) for w in range(2)]

    def response(i, _):
        for w, val in enumerate(grads(PC + i, i, 4)):
            for b in range(4):
                kv[b, w, pl.ds(mult(1024 + i * T, T), T), :] = val[b * T:(b + 1) * T]
        return 0

    scaled(4)
    lax.fori_loop(0, 4, response, 0)
    yback = []
    for d in (2, 1, 3):
        ty = (y + d) % 4
        copy = remote(kv.at[ty, :, pl.ds(1024, 512), :], rbuf.at[d - 1, :, pl.ds(1024, 512), :], ydev(d))
        copy.start()
        yback.append(copy)
    for d in (2, 1, 3, 0):
        ty = (y + d) % 4
        came = (4 - d) % 4
        scaled(order.index(came))

        def prefix(half, _):
            for w, val in enumerate(grads(came * 2 + half, 0, order.index(came))):
                kv[ty, w, pl.ds(mult(half * CH, CH), CH), :] = val
            return 0

        lax.fori_loop(0, 2, prefix, 0)
        if d:
            copy = remote(kv.at[ty, :, pl.ds(0, 1024), :], rbuf.at[d - 1, :, pl.ds(0, 1024), :], ydev(d))
            copy.start()
            yback.append(copy)

    for i in range(4):
        for h in range(HEADS):
            rs = slice(h * T, (h + 1) * T)
            dq_ref[i, :, rs] = (acc[i, rs, :T] * acc[i, rs, T:]).astype(BF)
    for d in range(4):
        tx = (x + d) % 4
        copy = local if d == 0 else functools.partial(remote, dev=xdev(d))
        homes.append(copy(dq_ref.at[tx], query_grad.at[resp, :, wide(kvh)]))
        homes[-1].start()

    for copy in yback:
        copy.wait()

    def total(b, _):
        for w in range(2):
            rs = pl.ds(mult(b * T, T), T)
            acc4 = kv[y, w, rs, :].astype(F32)
            for d in range(3):
                acc4 = acc4 + rbuf[d, w, rs, :].astype(F32)
            kv[y, w, rs, :] = acc4.astype(BF)
        return 0

    lax.fori_loop(0, 12, total, 0)
    tail = []
    for other in (1, 0):
        for d in range(4):
            tx, tg = (x + d) % 4, (grp + other) % 2
            copy = local if (d == 0 and not other) else functools.partial(remote, dev=xdev(d, other))
            tail.append(copy(kv.at[y, :, blk(tg * 4 + tx), :], pbuf.at[grp * 4 + x]))
    for d in range(4):
        tx = (x + d) % 4
        copy = local if d == 0 else functools.partial(remote, dev=xdev(d))
        for w, out in ((0, key_grad), (1, value_grad)):
            homes.append(copy(kv.at[y, w, blk(8 + tx), :], out.at[resp, :, hd(kvh)]))
            tail.append(homes.pop())
    for copy in tail:
        copy.start()
    for copy in tail[:8]:
        copy.wait()
    for j in range(2):
        for w, out in ((0, pk_grad), (1, pv_grad)):
            parts = [pbuf[gg * 4 + rr * 2 + j, w].astype(F32) for gg in range(2) for rr in range(2)]
            out[:, j * T:(j + 1) * T] = (parts[0] + parts[1] + parts[2] + parts[3]).astype(BF)
    for copy in tail[8:] + homes:
        copy.wait()
    assert counter[0] <= N_SEM and counter[1] <= N_SEM


def shards(queries, keys, values, prefix_keys, shared_prompt_values, lengths, grad_out):
    like = lambda a: jax.ShapeDtypeStruct(a.shape, BF)
    hbm = pl.BlockSpec(memory_space=pl.ANY)
    vmem = pl.BlockSpec(memory_space=pltpu.VMEM)
    V = pltpu.VMEM
    return pl.pallas_call(
        kernel,
        out_shape=[like(queries), like(queries), like(keys), like(keys), like(prefix_keys), like(prefix_keys)],
        in_specs=[pl.BlockSpec(memory_space=pltpu.SMEM)] + [hbm] * 6,
        out_specs=[hbm] * 4 + [vmem] * 2,
        scratch_shapes=[
            V((4, T, R), BF), V((4, T, R), BF), V((4, 2, 1536, T), BF), V((3, 2, 1536, T), BF),
            V((8, 2, T, T), BF), V((4, T, R), BF), V((4, T, R), BF),
            V((6144, 256), BF), V((6144, 256), BF), V((4, R, 256), BF), V((4, R, 256), BF),
            V((2, 4, T, R), BF), V((2, 4, T, R), BF), V((4, R, CH), F32), V((42, R, CH), BF),
            V((4, R, T), F32), V((4, R, T), F32), V((4, 8, R), F32), V((R, T), F32), V((4, R, 256), F32),
            pltpu.SemaphoreType.DMA((N_SEM,)), pltpu.SemaphoreType.DMA((N_SEM,)),
            pltpu.SemaphoreType.DMA((N_SEM,)),
        ],
        compiler_params=pltpu.CompilerParams(
            collective_id=0, has_side_effects=True, vmem_limit_bytes=64 * 1024 * 1024
        ),
        name="attention",
    )(lengths, queries, keys, values, prefix_keys, shared_prompt_values, grad_out)


def solution(mesh):
    acts, prompt = P("grp", "ctx", "head"), P(("grp", "ctx"), "head")
    return jax.shard_map(
        shards,
        mesh=mesh,
        in_specs=(acts, acts, acts, prompt, prompt, P("grp"), acts),
        out_specs=(acts, acts, acts, acts, prompt, prompt),
        check_vma=False,
    )
```

```python
import functools
import math

import jax
import jax.numpy as jnp
from jax import lax
from jax.experimental import pallas as pl
from jax.experimental.pallas import tpu as pltpu
from jax.sharding import PartitionSpec as P

MESH = pl.DeviceIdType.MESH
F32, BF = jnp.float32, jnp.bfloat16
T = 128
CH = 512
HEADS = 5
R = HEADS * T
PC = 8
NT = (((1,), (1,)), ((), ()))
NN = (((1,), (0,)), ((), ()))
dot = functools.partial(lax.dot_general, preferred_element_type=F32)
N_SEM = 64


def mult(v, n):
    return pl.multiple_of(v, n)


def kernel(
    lens_ref, queries, keys, values, pkeys, pvalues, gout,
    attended, query_grad, key_grad, value_grad, pk_grad, pv_grad,
    q_ref, g_ref, kv, rbuf, pbuf,
    ka, va, qa, gt, gs, s_ref, ds_ref, e_ref, mrun, stat, turned, top_ref, acc,
    send, recv, lsem,
):
    grp, ctx, head = lax.axis_index("grp"), lax.axis_index("ctx"), lax.axis_index("head")
    x, y = ctx // 4, ctx % 4
    resp, kvh = x // 2, x % 2
    c2 = 1.4426950408889634 / math.sqrt(T)
    scale = 1.0 / math.sqrt(T)

    def xdev(d, other=0):
        return ((grp + other) % 2, ((x + d) % 4) * 4 + y, head)

    def ydev(d):
        return (grp, x * 4 + (y + d) % 4, head)

    counter = [0, 0]

    def remote(src, dst, dev):
        k = counter[0]
        counter[0] += 1
        return pltpu.make_async_remote_copy(
            src_ref=src, dst_ref=dst, send_sem=send.at[k], recv_sem=recv.at[k],
            device_id=dev, device_id_type=MESH,
        )

    def local(src, dst):
        k = counter[1]
        counter[1] += 1
        return pltpu.make_async_copy(src, dst, lsem.at[k])

    partners = [xdev(d) for d in (1, 2, 3)] + [ydev(d) for d in (1, 2, 3)] + [xdev(d, 1) for d in range(4)]
    barrier = pltpu.get_barrier_semaphore()
    for dev in partners:
        pl.semaphore_signal(barrier, inc=1, device_id=dev, device_id_type=MESH)
    pl.semaphore_wait(barrier, len(partners))

    def hd(j):
        return pl.ds(mult(j * T, T), T)

    def wide(j):
        return pl.ds(mult(j * R, T), R)

    def blk(b):
        return pl.ds(mult(b * T, T), T)

    pre, own, late = [], [], []
    for other in (0, 1):
        for d in range(4):
            tx = (x + d) % 4
            j = tx % 2
            here = d == 0 and not other
            copy = local if here else functools.partial(remote, dev=xdev(d, other))
            for which, ref in ((0, pkeys), (1, pvalues)):
                pre.append(copy(ref.at[:, hd(j)], kv.at[y, which, blk(grp * 4 + x), :]))
    for d in range(4):
        tx = (x + d) % 4
        r, j = tx // 2, tx % 2
        copy = local if d == 0 else functools.partial(remote, dev=xdev(d))
        for which, ref in ((0, keys), (1, values)):
            pre.append(copy(ref.at[r, :, hd(j)], kv.at[y, which, blk(8 + x), :]))
        for ref, buf in ((queries, q_ref), (gout, g_ref)):
            (late if d else own).append(copy(ref.at[r, :, wide(j)], buf.at[x]))
    for copy in pre + own:
        copy.start()
    for copy in own + pre:
        copy.wait()
    asked, graded = late[0::2], late[1::2]
    for copy in asked:
        copy.start()

    front, back = pl.ds(0, 1024), pl.ds(1024, 512)

    def near(rows):
        return [remote(kv.at[y, :, rows, :], kv.at[y, :, rows, :], ydev(d)) for d in (1, 3)]

    def far(rows):
        up, down = (y + 1) % 4, (y + 3) % 4
        return [
            remote(kv.at[up, 0, rows, :], kv.at[up, 0, rows, :], ydev(3)),
            remote(kv.at[down, 1, rows, :], kv.at[down, 1, rows, :], ydev(1)),
        ]

    near_front, near_back, far_front, far_back = near(front), near(back), far(front), far(back)
    for copy in near_front:
        copy.start()

    def place(d):
        sy = (y - d) % 4
        ps = pl.ds(d * 1024, 1024)
        ka[ps, :T] = kv[sy, 0, :1024, :]
        ka[ps, T:] = kv[sy, 0, :1024, :]
        va[ps, :T] = kv[sy, 1, :1024, :]
        va[ps, T:] = jnp.ones((1024, T), BF)

    def place_response():
        for sy in range(4):
            for i in range(4):
                rs = slice(4096 + i * CH + sy * T, 4096 + i * CH + (sy + 1) * T)
                src = slice(1024 + i * T, 1024 + (i + 1) * T)
                ka[rs, :T] = kv[sy, 0, src, :]
                ka[rs, T:] = kv[sy, 0, src, :]
                va[rs, :T] = kv[sy, 1, src, :]
                va[rs, T:] = jnp.ones((T, T), BF)

    def slot(c, i):
        n = c - PC
        return jnp.where(n < 0, 4 * c + i, 32 + 4 * n - (n * (n - 1)) // 2 + i - n)

    def chunk_rows(c):
        return pl.ds(mult(c * CH, CH), CH)

    def fold(s):
        return functools.reduce(jnp.maximum, [s[:, k * T:(k + 1) * T] for k in range(CH // T)])

    lane = lax.broadcasted_iota(jnp.int32, (R, T), 1)

    def prepare(i, _):
        for h in range(HEADS):
            rs = slice(h * T, (h + 1) * T)
            qs = q_ref[i, :, rs].astype(F32) * c2
            hi = qs.astype(BF)
            qa[i, rs, :T] = hi
            qa[i, rs, T:] = (qs - hi.astype(F32)).astype(BF)
        acc[i] = jnp.zeros((R, 2 * T), F32)
        mrun[i] = jnp.full((R, T), -jnp.inf, F32)
        stat[i] = jnp.zeros((R, T), F32)
        return 0

    def scores(i, c, slot):
        s = dot(qa[i], ka[chunk_rows(c), :], NT)
        s_ref[slot] = s
        return fold(s)

    def weigh(i, base, count, g, top):
        old = mrun[i]
        new = jnp.maximum(old, jnp.broadcast_to(jnp.max(top, 1, keepdims=True), (R, T)))
        mrun[i] = new
        stat[i] = jnp.where(lane == g, new, stat[i])
        fade = jnp.exp2(old - new)
        acc[i, :, :T] *= fade
        acc[i, :, T:] *= fade

        def exps(n, _):
            c = base + n
            mm = mrun[i]
            s = s_ref[n]
            e = jnp.concatenate(
                [jnp.exp2(s[:, k * T:(k + 1) * T] - mm) for k in range(CH // T)], 1
            ).astype(BF)
            e_ref[slot(c, i)] = e
            acc[i] += dot(e, va[chunk_rows(c), :], NN)
            return 0

        lax.fori_loop(0, count, exps, 0)

    def prefix_tile(i, d, g):
        top = jnp.maximum(scores(i, 2 * d, 0), scores(i, 2 * d + 1, 1))
        weigh(i, 2 * d, 2, g, top)

    def prefix_group(d, g, first):
        def tile(n, _):
            prefix_tile((x + n) % 4, d, g)
            return 0

        lax.fori_loop(first, 4, tile, 0)

    def response_tile(i, _):
        top_ref[...] = jnp.full((R, T), -jnp.inf, F32)

        def one(n, _):
            top_ref[...] = jnp.maximum(top_ref[...], scores(i, PC + n, n))
            return 0

        lax.fori_loop(0, i, one, 0)
        s = dot(qa[i], ka[chunk_rows(PC + i), :], NT)
        col = lax.broadcasted_iota(jnp.int32, (T, CH), 1)
        row = lax.broadcasted_iota(jnp.int32, (T, CH), 0) + y * T
        seen = col <= row
        s = jnp.concatenate(
            [jnp.where(seen, s[h * T:(h + 1) * T], -jnp.inf) for h in range(HEADS)], 0
        )
        s_ref[i] = s
        weigh(i, PC, i + 1, 4, jnp.maximum(top_ref[...], fold(s)))
        stat[i] = jnp.exp2(stat[i] - mrun[i])
        pos = lax.broadcasted_iota(jnp.int32, (T, T), 0) + (i * CH + y * T)
        live = pos < lens_ref[resp]
        part = lax.broadcasted_iota(jnp.int32, (T, T), 1)
        for h in range(HEADS):
            rs = slice(h * T, (h + 1) * T)
            inv = 1.0 / acc[i, rs, T:]
            o = jnp.where(live, acc[i, rs, :T] * inv, 0.0).astype(BF)
            g = jnp.where(live, g_ref[i, :, rs].astype(F32), 0.0)
            g_ref[i, :, rs] = o
            d0 = -jnp.sum(g * o.astype(F32), 1, keepdims=True)
            d1 = d0.astype(BF).astype(F32)
            d2 = (d0 - d1).astype(BF).astype(F32)
            d3 = d0 - d1 - d2
            qa[i, rs, :T] = g.astype(BF)
            qa[i, rs, T:] = jnp.where(
                part == 0, d1, jnp.where(part == 1, d2, jnp.where(part == 2, d3, 0.0))
            ).astype(BF)
            gt[0, i, :, rs] = (q_ref[i, :, rs].astype(F32) * (inv * scale)).astype(BF).T
            gt[1, i, :, rs] = (g * inv).astype(BF).T
            turned[i, :, rs] = stat[i, rs, :].T[:8]
            acc[i, rs, T:] = inv * scale
        acc[i, :, :T] = jnp.zeros((R, T), F32)
        return 0

    order = (0, 1, 3, 2)
    place(0)
    prepare(x, 0)
    prefix_tile(x, 0, 0)
    for copy in asked:
        copy.wait()
    for copy in graded:
        copy.start()
    lax.fori_loop(1, 4, lambda n, _: prepare((x + n) % 4, 0), 0)
    prefix_group(0, 0, 1)
    for copy in near_front:
        copy.wait()
    for copy in far_front + near_back:
        copy.start()
    for g in (1, 2):
        place(order[g])
        prefix_group(order[g], g, 0)
    for copy in near_back:
        copy.wait()
    for copy in far_back:
        copy.start()
    for copy in far_front:
        copy.wait()
    place(2)
    prefix_group(2, 3, 0)
    for copy in far_back + graded:
        copy.wait()
    place_response()
    lax.fori_loop(0, 4, response_tile, 0)

    homes = []
    for d in range(4):
        tx = (x + d) % 4
        copy = local if d == 0 else functools.partial(remote, dev=xdev(d))
        homes.append(copy(g_ref.at[tx], attended.at[resp, :, wide(kvh)]))
    for copy in homes:
        copy.start()

    def scaled(g):
        for i in range(4):
            f = turned[i, g:g + 1, :]
            for w in range(2):
                gs[w, :, i * R:(i + 1) * R] = (gt[w, i].astype(F32) * f).astype(BF)

    def rows_part(i, c, g, buf):
        kk = chunk_rows(c)
        dp = dot(qa[i], va[kk, :], NT)
        ds = (e_ref[slot(c, i)].astype(F32) * dp).astype(BF)
        ds_ref[buf, i] = ds
        acc[i, :, :T] += stat[i, :, g:g + 1] * dot(ds, ka[kk, :T], NN)

    def keys_part(c, first, buf):
        n = (4 - first) * R
        base = slot(c, first)
        ds = ds_ref[buf, first:].reshape(n, CH)
        e = e_ref[pl.ds(base, 4 - first)].reshape(n, CH)
        dk = dot(gs[0, :, first * R:], ds, NN)
        dv = dot(gs[1, :, first * R:], e, NN)
        return dk.T.astype(BF), dv.T.astype(BF)

    def all_rows(c, first, g, buf):
        lax.fori_loop(first, 4, lambda i, _: (rows_part(i, c, g, buf), 0)[1], 0)

    scaled(4)
    for i in range(4):
        all_rows(PC + i, i, 4, 0)
        for w, val in enumerate(keys_part(PC + i, i, 0)):
            for b in range(4):
                kv[b, w, 1024 + i * T:1024 + (i + 1) * T, :] = val[b * T:(b + 1) * T]
    yback_resp, yback = [], []
    for d in (2, 1, 3):
        ty = (y + d) % 4
        yback_resp.append(remote(kv.at[ty, :, back, :], rbuf.at[d - 1, :, back, :], ydev(d)))
        yback_resp[-1].start()

    def total(b, _):
        for w in range(2):
            rs = pl.ds(mult(b * T, T), T)
            acc4 = kv[y, w, rs, :].astype(F32)
            for d in range(3):
                acc4 = acc4 + rbuf[d, w, rs, :].astype(F32)
            kv[y, w, rs, :] = acc4.astype(BF)
        return 0

    for d in (2, 1, 3, 0):
        ty = (y + d) % 4
        came = (4 - d) % 4
        g = order.index(came)
        scaled(g)

        def finish(half, _):
            for w, val in enumerate(keys_part(came * 2 + half, 0, half)):
                kv[ty, w, pl.ds(mult(half * CH, CH), CH), :] = val
            return 0

        def both(half, _):
            all_rows(came * 2 + half, 0, g, half)
            return 0

        lax.fori_loop(0, 2, both, 0)
        if d == 0:
            for i in range(4):
                for h in range(HEADS):
                    rs = slice(h * T, (h + 1) * T)
                    q_ref[i, :, rs] = (acc[i, rs, :T] * acc[i, rs, T:]).astype(BF)
            for e in (2, 1, 3, 0):
                tx = (x + e) % 4
                copy = local if e == 0 else functools.partial(remote, dev=xdev(e))
                homes.append(copy(q_ref.at[tx], query_grad.at[resp, :, wide(kvh)]))
                homes[-1].start()
        lax.fori_loop(0, 2, finish, 0)
        if d:
            yback.append(remote(kv.at[ty, :, front, :], rbuf.at[d - 1, :, front, :], ydev(d)))
            yback[-1].start()
        if d == 3:
            for copy in yback_resp:
                copy.wait()
            lax.fori_loop(8, 12, total, 0)
            for e in range(4):
                tx = (x + e) % 4
                copy = local if e == 0 else functools.partial(remote, dev=xdev(e))
                for w, out in ((0, key_grad), (1, value_grad)):
                    homes.append(copy(kv.at[y, w, blk(8 + tx), :], out.at[resp, :, hd(kvh)]))
                    homes[-1].start()

    for copy in yback:
        copy.wait()
    lax.fori_loop(0, 8, total, 0)
    tail = []
    for other in (1, 0):
        for d in (2, 1, 3, 0):
            tx, tg = (x + d) % 4, (grp + other) % 2
            copy = local if (d == 0 and not other) else functools.partial(remote, dev=xdev(d, other))
            tail.append(copy(kv.at[y, :, blk(tg * 4 + tx), :], pbuf.at[grp * 4 + x]))
            tail[-1].start()
    for copy in tail:
        copy.wait()
    for j in range(2):
        for w, out in ((0, pk_grad), (1, pv_grad)):
            parts = [pbuf[gg * 4 + rr * 2 + j, w].astype(F32) for gg in range(2) for rr in range(2)]
            out[:, j * T:(j + 1) * T] = (parts[0] + parts[1] + parts[2] + parts[3]).astype(BF)
    for copy in homes:
        copy.wait()
    assert counter[0] <= N_SEM and counter[1] <= N_SEM


def settle(*refs):
    n = len(refs) // 3
    arrived, left = refs[3 * n:]
    loads = [pltpu.make_async_copy(refs[k], refs[2 * n + k], arrived.at[k]) for k in range(n)]
    stores = [pltpu.make_async_copy(refs[2 * n + k], refs[n + k], left.at[k]) for k in range(n)]
    for copy in loads:
        copy.start()
    for load, store in zip(loads, stores):
        load.wait()
        store.start()
    for copy in stores:
        copy.wait()


def shards(queries, keys, values, prefix_keys, shared_prompt_values, lengths, grad_out):
    like = lambda a: jax.ShapeDtypeStruct(a.shape, BF)
    hbm = pl.BlockSpec(memory_space=pl.ANY)
    vmem = pl.BlockSpec(memory_space=pltpu.VMEM)
    V = pltpu.VMEM
    shapes = [like(queries), like(queries), like(keys), like(keys), like(prefix_keys), like(prefix_keys)]
    made = pl.pallas_call(
        kernel,
        out_shape=shapes,
        in_specs=[pl.BlockSpec(memory_space=pltpu.SMEM)] + [hbm] * 6,
        out_specs=[hbm] * 4 + [vmem] * 2,
        scratch_shapes=[
            V((4, T, R), BF), V((4, T, R), BF), V((4, 2, 1536, T), BF), V((3, 2, 1536, T), BF),
            V((8, 2, T, T), BF),
            V((6144, 256), BF), V((6144, 256), BF), V((4, R, 256), BF),
            V((2, 4, T, R), BF), V((2, T, 4 * R), BF), V((4, R, CH), F32), V((2, 4, R, CH), BF), V((42, R, CH), BF),
            V((4, R, T), F32), V((4, R, T), F32), V((4, 8, R), F32), V((R, T), F32), V((4, R, 256), F32),
            pltpu.SemaphoreType.DMA((N_SEM,)), pltpu.SemaphoreType.DMA((N_SEM,)),
            pltpu.SemaphoreType.DMA((N_SEM,)),
        ],
        compiler_params=pltpu.CompilerParams(
            collective_id=0, has_side_effects=True, vmem_limit_bytes=64 * 1024 * 1024
        ),
        name="attention",
    )(lengths, queries, keys, values, prefix_keys, shared_prompt_values, grad_out)
    return pl.pallas_call(
        settle,
        out_shape=shapes,
        in_specs=[hbm] * 6,
        out_specs=[hbm] * 6,
        scratch_shapes=[V(a.shape, BF) for a in shapes] + [pltpu.SemaphoreType.DMA((6,))] * 2,
        name="settle",
    )(*made)


def solution(mesh):
    acts, prompt = P("grp", "ctx", "head"), P(("grp", "ctx"), "head")
    return jax.shard_map(
        shards,
        mesh=mesh,
        in_specs=(acts, acts, acts, prompt, prompt, P("grp"), acts),
        out_specs=(acts, acts, acts, acts, prompt, prompt),
        check_vma=False,
    )
```

```python
import functools
import math

import jax
import jax.numpy as jnp
from jax import lax
from jax.experimental import pallas as pl
from jax.experimental.pallas import tpu as pltpu
from jax.sharding import PartitionSpec as P

MESH = pl.DeviceIdType.MESH
F32, BF = jnp.float32, jnp.bfloat16
T = 128
CH = 512
HEADS = 5
R = HEADS * T
PC = 8
NT = (((1,), (1,)), ((), ()))
NN = (((1,), (0,)), ((), ()))
dot = functools.partial(lax.dot_general, preferred_element_type=F32)
N_SEM = 64


def mult(v, n):
    return pl.multiple_of(v, n)


def kernel(
    lens_ref, queries, keys, values, pkeys, pvalues, gout,
    attended, query_grad, key_grad, value_grad, pk_grad, pv_grad,
    q_ref, g_ref, kv, rbuf, pbuf,
    ka, va, qa, gt, gs, s_ref, ds_ref, e_ref, mrun, stat, turned, top_ref, acc,
    send, recv, lsem,
):
    grp, ctx, head = lax.axis_index("grp"), lax.axis_index("ctx"), lax.axis_index("head")
    x, y = ctx // 4, ctx % 4
    resp, kvh = x // 2, x % 2
    c2 = 1.4426950408889634 / math.sqrt(T)
    scale = 1.0 / math.sqrt(T)

    def xdev(d, other=0):
        return ((grp + other) % 2, ((x + d) % 4) * 4 + y, head)

    def ydev(d):
        return (grp, x * 4 + (y + d) % 4, head)

    counter = [0, 0]

    def remote(src, dst, dev):
        k = counter[0]
        counter[0] += 1
        return pltpu.make_async_remote_copy(
            src_ref=src, dst_ref=dst, send_sem=send.at[k], recv_sem=recv.at[k],
            device_id=dev, device_id_type=MESH,
        )

    def local(src, dst):
        k = counter[1]
        counter[1] += 1
        return pltpu.make_async_copy(src, dst, lsem.at[k])

    partners = [xdev(d) for d in (1, 2, 3)] + [ydev(d) for d in (1, 2, 3)] + [xdev(d, 1) for d in range(4)]
    barrier = pltpu.get_barrier_semaphore()
    for dev in partners:
        pl.semaphore_signal(barrier, inc=1, device_id=dev, device_id_type=MESH)
    pl.semaphore_wait(barrier, len(partners))

    def hd(j):
        return pl.ds(mult(j * T, T), T)

    def wide(j):
        return pl.ds(mult(j * R, T), R)

    pre, own, late = [], [], []
    for d in range(4):
        j = (x + d) % 2
        copy = local if d == 0 else functools.partial(remote, dev=xdev(d))
        for which, ref in ((0, pkeys), (1, pvalues)):
            pre.append(copy(ref.at[:, hd(j)], kv.at[y, grp, x, which]))
    for d in range(4):
        tx = (x + d) % 4
        r, j = tx // 2, tx % 2
        copy = local if d == 0 else functools.partial(remote, dev=xdev(d))
        for which, ref in ((0, keys), (1, values)):
            pre.append(copy(ref.at[r, :, hd(j)], kv.at[y, 2, x, which]))
        for ref, buf in ((queries, q_ref), (gout, g_ref)):
            (late if d else own).append(copy(ref.at[r, :, wide(j)], buf.at[x]))
    for copy in pre + own:
        copy.start()
    asked, graded = late[0::2], late[1::2]

    up, down = (y + 1) % 4, (y + 3) % 4

    def near(part):
        return [remote(kv.at[y, part], kv.at[y, part], ydev(d)) for d in (1, 3)]

    def far(part):
        low, high = pl.ds(0, 2), pl.ds(2, 2)
        return [
            remote(kv.at[up, part, low], kv.at[up, part, low], ydev(3)),
            remote(kv.at[down, part, high], kv.at[down, part, high], ydev(1)),
        ]

    def across(d):
        sy = (y - d) % 4
        return [remote(kv.at[sy, grp], kv.at[sy, grp], xdev(0, 1))]

    near_prompt, near_resp, far_prompt, far_resp = near(grp), near(2), far(grp), far(2)
    swap = {d: across(d) for d in range(4)}

    def start(copies):
        for copy in copies:
            copy.start()

    def wait(copies):
        for copy in copies:
            copy.wait()

    wait(pre[:8])
    start(near_prompt + swap[0])
    wait(pre[8:])
    start(asked)

    OWN, OTHER = 0, 1
    uses = [(0, OWN), (0, OTHER), (1, OWN), (3, OWN), (1, OTHER), (2, OWN), (3, OTHER), (2, OTHER)]

    def half(kind):
        return (grp + kind) % 2

    def place(p):
        d, kind = uses[p]
        sy = (y - d) % 4
        for b in range(4):
            rs = slice(p * CH + b * T, p * CH + (b + 1) * T)
            ka[rs, :T] = kv[sy, half(kind), b, 0]
            ka[rs, T:] = kv[sy, half(kind), b, 0]
            va[rs, :T] = kv[sy, half(kind), b, 1]
            va[rs, T:] = jnp.ones((T, T), BF)

    def place_response():
        for sy in range(4):
            for i in range(4):
                rs = slice(4096 + i * CH + sy * T, 4096 + i * CH + (sy + 1) * T)
                ka[rs, :T] = kv[sy, 2, i, 0]
                ka[rs, T:] = kv[sy, 2, i, 0]
                va[rs, :T] = kv[sy, 2, i, 1]
                va[rs, T:] = jnp.ones((T, T), BF)

    def slot(c, i):
        n = c - PC
        return jnp.where(n < 0, 4 * c + i, 32 + 4 * n - (n * (n - 1)) // 2 + i - n)

    def chunk_rows(c):
        return pl.ds(mult(c * CH, CH), CH)

    def fold(s):
        return functools.reduce(jnp.maximum, [s[:, k * T:(k + 1) * T] for k in range(CH // T)])

    lane = lax.broadcasted_iota(jnp.int32, (R, T), 1)

    def prepare(i, _):
        for h in range(HEADS):
            rs = slice(h * T, (h + 1) * T)
            qs = q_ref[i, :, rs].astype(F32) * c2
            hi = qs.astype(BF)
            qa[i, rs, :T] = hi
            qa[i, rs, T:] = (qs - hi.astype(F32)).astype(BF)
        acc[i] = jnp.zeros((R, 2 * T), F32)
        mrun[i] = jnp.full((R, T), -jnp.inf, F32)
        stat[i] = jnp.zeros((R, T), F32)
        return 0

    def scores(i, c, slot):
        s = dot(qa[i], ka[chunk_rows(c), :], NT)
        s_ref[slot] = s
        return fold(s)

    def weigh(i, base, count, g, top):
        old = mrun[i]
        new = jnp.maximum(old, jnp.broadcast_to(jnp.max(top, 1, keepdims=True), (R, T)))
        mrun[i] = new
        stat[i] = jnp.where(lane == g, new, stat[i])
        fade = jnp.exp2(old - new)
        acc[i, :, :T] *= fade
        acc[i, :, T:] *= fade

        def exps(n, _):
            c = base + n
            mm = mrun[i]
            s = s_ref[n]
            e = jnp.concatenate(
                [jnp.exp2(s[:, k * T:(k + 1) * T] - mm) for k in range(CH // T)], 1
            ).astype(BF)
            e_ref[slot(c, i)] = e
            acc[i] += dot(e, va[chunk_rows(c), :], NN)
            return 0

        lax.fori_loop(0, count, exps, 0)

    def prefix_group(g):
        place(2 * g)
        place(2 * g + 1)

        def tile(i, _):
            top = jnp.maximum(scores(i, 2 * g, 0), scores(i, 2 * g + 1, 1))
            weigh(i, 2 * g, 2, g, top)
            return 0

        lax.fori_loop(0, 4, tile, 0)

    def response_tile(i, _):
        top_ref[...] = jnp.full((R, T), -jnp.inf, F32)

        def one(n, _):
            top_ref[...] = jnp.maximum(top_ref[...], scores(i, PC + n, n))
            return 0

        lax.fori_loop(0, i, one, 0)
        s = dot(qa[i], ka[chunk_rows(PC + i), :], NT)
        col = lax.broadcasted_iota(jnp.int32, (T, CH), 1)
        row = lax.broadcasted_iota(jnp.int32, (T, CH), 0) + y * T
        seen = col <= row
        s = jnp.concatenate(
            [jnp.where(seen, s[h * T:(h + 1) * T], -jnp.inf) for h in range(HEADS)], 0
        )
        s_ref[i] = s
        weigh(i, PC, i + 1, 4, jnp.maximum(top_ref[...], fold(s)))
        stat[i] = jnp.exp2(stat[i] - mrun[i])
        pos = lax.broadcasted_iota(jnp.int32, (T, T), 0) + (i * CH + y * T)
        live = pos < lens_ref[resp]
        part = lax.broadcasted_iota(jnp.int32, (T, T), 1)
        for h in range(HEADS):
            rs = slice(h * T, (h + 1) * T)
            inv = 1.0 / acc[i, rs, T:]
            o = jnp.where(live, acc[i, rs, :T] * inv, 0.0).astype(BF)
            g = jnp.where(live, g_ref[i, :, rs].astype(F32), 0.0)
            g_ref[i, :, rs] = o
            d0 = -jnp.sum(g * o.astype(F32), 1, keepdims=True)
            d1 = d0.astype(BF).astype(F32)
            d2 = (d0 - d1).astype(BF).astype(F32)
            d3 = d0 - d1 - d2
            qa[i, rs, :T] = g.astype(BF)
            qa[i, rs, T:] = jnp.where(
                part == 0, d1, jnp.where(part == 1, d2, jnp.where(part == 2, d3, 0.0))
            ).astype(BF)
            gt[0, i, :, rs] = (q_ref[i, :, rs].astype(F32) * (inv * scale)).astype(BF).T
            gt[1, i, :, rs] = (g * inv).astype(BF).T
            turned[i, :, rs] = stat[i, rs, :].T[:8]
            acc[i, rs, T:] = inv * scale
        acc[i, :, :T] = jnp.zeros((R, T), F32)
        return 0

    wait(own + asked)
    start(graded)
    lax.fori_loop(0, 4, prepare, 0)
    wait(near_prompt + swap[0])
    start(swap[1] + far_prompt + near_resp)
    prefix_group(0)
    wait(swap[1])
    start(swap[3])
    prefix_group(1)
    wait(far_prompt)
    start(swap[2])
    wait(near_resp)
    start(far_resp)
    prefix_group(2)
    wait(swap[3] + swap[2])
    prefix_group(3)
    wait(far_resp + graded)
    place_response()
    lax.fori_loop(0, 4, response_tile, 0)

    homes = []
    for d in range(4):
        tx = (x + d) % 4
        copy = local if d == 0 else functools.partial(remote, dev=xdev(d))
        homes.append(copy(g_ref.at[tx], attended.at[resp, :, wide(kvh)]))
    for copy in homes:
        copy.start()

    def scaled(g):
        for i in range(4):
            f = turned[i, g:g + 1, :]
            for w in range(2):
                gs[w, :, i * R:(i + 1) * R] = (gt[w, i].astype(F32) * f).astype(BF)

    def rows_part(i, c, g):
        kk = chunk_rows(c)
        dp = dot(qa[i], va[kk, :], NT)
        ds = (e_ref[slot(c, i)].astype(F32) * dp).astype(BF)
        ds_ref[i] = ds
        acc[i, :, :T] += stat[i, :, g:g + 1] * dot(ds, ka[kk, :T], NN)

    def keys_part(c, first):
        n = (4 - first) * R
        base = slot(c, first)
        ds = ds_ref[first:].reshape(n, CH)
        e = e_ref[pl.ds(base, 4 - first)].reshape(n, CH)
        dk = dot(gs[0, :, first * R:], ds, NN)
        dv = dot(gs[1, :, first * R:], e, NN)
        return dk.T.astype(BF), dv.T.astype(BF)

    def all_rows(c, first, g):
        lax.fori_loop(first, 4, lambda i, _: (rows_part(i, c, g), 0)[1], 0)

    scaled(4)
    for i in range(4):
        all_rows(PC + i, i, 4)
        for w, val in enumerate(keys_part(PC + i, i)):
            for b in range(4):
                kv[b, 2, i, w] = val[b * T:(b + 1) * T]

    def send_back(d, part):
        ty = (y + d) % 4
        copy = remote(kv.at[ty, part], rbuf.at[d - 1, part], ydev(d))
        copy.start()
        return copy

    def total(part):
        def block(b, _):
            for w in range(2):
                acc4 = kv[y, part, b, w].astype(F32)
                for d in range(3):
                    acc4 = acc4 + rbuf[d, part, b, w].astype(F32)
                kv[y, part, b, w] = acc4.astype(BF)
            return 0

        lax.fori_loop(0, 4, block, 0)

    yback = {2: [send_back(d, 2) for d in (2, 1, 3)], OTHER: [], OWN: []}
    tail = []
    for kind in (OTHER, OWN):
        for d in (2, 1, 3, 0):
            p = uses.index(((4 - d) % 4, kind))
            ty, part = (y + d) % 4, half(kind)
            scaled(p // 2)
            all_rows(p, 0, p // 2)
            if d == 0 and kind == OWN:
                for i in range(4):
                    for h in range(HEADS):
                        rs = slice(h * T, (h + 1) * T)
                        q_ref[i, :, rs] = (acc[i, rs, :T] * acc[i, rs, T:]).astype(BF)
                for e in (2, 1, 3, 0):
                    tx = (x + e) % 4
                    copy = local if e == 0 else functools.partial(remote, dev=xdev(e))
                    homes.append(copy(q_ref.at[tx], query_grad.at[resp, :, wide(kvh)]))
                    homes[-1].start()
            for w, val in enumerate(keys_part(p, 0)):
                for b in range(4):
                    kv[ty, part, b, w] = val[b * T:(b + 1) * T]
            if d:
                yback[kind].append(send_back(d, part))
            if d == 3 and kind == OTHER:
                wait(yback[2])
                total(2)
                for e in range(4):
                    tx = (x + e) % 4
                    copy = local if e == 0 else functools.partial(remote, dev=xdev(e))
                    for w, out in ((0, key_grad), (1, value_grad)):
                        homes.append(copy(kv.at[y, 2, tx, w], out.at[resp, :, hd(kvh)]))
                        homes[-1].start()
            if d == 2 and kind == OWN:
                wait(yback[OTHER])
                total(half(OTHER))
                for e in (2, 1, 3, 0):
                    tail.append(remote(kv.at[y, half(OTHER), (x + e) % 4], pbuf.at[grp * 4 + x], xdev(e, 1)))
                    tail[-1].start()

    wait(yback[OWN])
    total(half(OWN))
    for e in (2, 1, 3):
        tail.append(remote(kv.at[y, grp, (x + e) % 4], pbuf.at[grp * 4 + x], xdev(e)))
        tail[-1].start()
    pbuf[grp * 4 + x] = kv[y, grp, x]
    wait(tail)
    for j in range(2):
        for w, out in ((0, pk_grad), (1, pv_grad)):
            parts = [pbuf[gg * 4 + rr * 2 + j, w].astype(F32) for gg in range(2) for rr in range(2)]
            out[:, j * T:(j + 1) * T] = (parts[0] + parts[1] + parts[2] + parts[3]).astype(BF)
    wait(homes)
    assert counter[0] <= N_SEM and counter[1] <= N_SEM


def settle(*refs):
    n = len(refs) // 3
    arrived, left = refs[3 * n:]
    loads = [pltpu.make_async_copy(refs[k], refs[2 * n + k], arrived.at[k]) for k in range(n)]
    stores = [pltpu.make_async_copy(refs[2 * n + k], refs[n + k], left.at[k]) for k in range(n)]
    for copy in loads:
        copy.start()
    for load, store in zip(loads, stores):
        load.wait()
        store.start()
    for copy in stores:
        copy.wait()


def shards(queries, keys, values, prefix_keys, shared_prompt_values, lengths, grad_out):
    like = lambda a: jax.ShapeDtypeStruct(a.shape, BF)
    hbm = pl.BlockSpec(memory_space=pl.ANY)
    vmem = pl.BlockSpec(memory_space=pltpu.VMEM)
    V = pltpu.VMEM
    shapes = [like(queries), like(queries), like(keys), like(keys), like(prefix_keys), like(prefix_keys)]
    made = pl.pallas_call(
        kernel,
        out_shape=shapes,
        in_specs=[pl.BlockSpec(memory_space=pltpu.SMEM)] + [hbm] * 6,
        out_specs=[hbm] * 4 + [vmem] * 2,
        scratch_shapes=[
            V((4, T, R), BF), V((4, T, R), BF), V((4, 3, 4, 2, T, T), BF), V((3, 3, 4, 2, T, T), BF),
            V((8, 2, T, T), BF),
            V((6144, 256), BF), V((6144, 256), BF), V((4, R, 256), BF),
            V((2, 4, T, R), BF), V((2, T, 4 * R), BF), V((4, R, CH), F32), V((4, R, CH), BF), V((42, R, CH), BF),
            V((4, R, T), F32), V((4, R, T), F32), V((4, 8, R), F32), V((R, T), F32), V((4, R, 256), F32),
            pltpu.SemaphoreType.DMA((N_SEM,)), pltpu.SemaphoreType.DMA((N_SEM,)),
            pltpu.SemaphoreType.DMA((N_SEM,)),
        ],
        compiler_params=pltpu.CompilerParams(
            collective_id=0, has_side_effects=True, vmem_limit_bytes=64 * 1024 * 1024
        ),
        name="attention",
    )(lengths, queries, keys, values, prefix_keys, shared_prompt_values, grad_out)
    return pl.pallas_call(
        settle,
        out_shape=shapes,
        in_specs=[hbm] * 6,
        out_specs=[hbm] * 6,
        scratch_shapes=[V(a.shape, BF) for a in shapes] + [pltpu.SemaphoreType.DMA((6,))] * 2,
        name="settle",
    )(*made)


def solution(mesh):
    acts, prompt = P("grp", "ctx", "head"), P(("grp", "ctx"), "head")
    return jax.shard_map(
        shards,
        mesh=mesh,
        in_specs=(acts, acts, acts, prompt, prompt, P("grp"), acts),
        out_specs=(acts, acts, acts, acts, prompt, prompt),
        check_vma=False,
    )
```

```python
import functools
import math

import jax
import jax.numpy as jnp
from jax import lax
from jax.experimental import pallas as pl
from jax.experimental.pallas import tpu as pltpu
from jax.sharding import PartitionSpec as P

MESH = pl.DeviceIdType.MESH
F32, BF = jnp.float32, jnp.bfloat16
T = 128
CH = 512
HEADS = 5
R = HEADS * T
PC = 8
NT = (((1,), (1,)), ((), ()))
NN = (((1,), (0,)), ((), ()))
dot = functools.partial(lax.dot_general, preferred_element_type=F32)
N_SEM = 64


def mult(v, n):
    return pl.multiple_of(v, n)


def kernel(
    lens_ref, queries, keys, values, pkeys, pvalues, gout,
    attended, query_grad, key_grad, value_grad, pk_grad, pv_grad,
    q_ref, g_ref, kv, rbuf, zbuf, pbuf,
    ka, va, qa, gt, gs, s_ref, ds_ref, e_ref, mrun, stat, turned, acc,
    send, recv, lsem,
):
    grp, ctx, head = lax.axis_index("grp"), lax.axis_index("ctx"), lax.axis_index("head")
    x, y = ctx // 4, ctx % 4
    resp, kvh = x // 2, x % 2
    c2 = 1.4426950408889634 / math.sqrt(T)
    scale = 1.0 / math.sqrt(T)

    def xdev(d, other=0):
        return ((grp + other) % 2, ((x + d) % 4) * 4 + y, head)

    def ydev(d):
        return (grp, x * 4 + (y + d) % 4, head)

    counter = [0, 0]

    def remote(src, dst, dev):
        k = counter[0]
        counter[0] += 1
        return pltpu.make_async_remote_copy(
            src_ref=src, dst_ref=dst, send_sem=send.at[k], recv_sem=recv.at[k],
            device_id=dev, device_id_type=MESH,
        )

    def local(src, dst):
        k = counter[1]
        counter[1] += 1
        return pltpu.make_async_copy(src, dst, lsem.at[k])

    partners = [xdev(d) for d in (1, 2, 3)] + [ydev(d) for d in (1, 2, 3)] + [xdev(0, 1)]
    barrier = pltpu.get_barrier_semaphore()
    for dev in partners:
        pl.semaphore_signal(barrier, inc=1, device_id=dev, device_id_type=MESH)
    pl.semaphore_wait(barrier, len(partners))

    def hd(j):
        return pl.ds(mult(j * T, T), T)

    def wide(j):
        return pl.ds(mult(j * R, T), R)

    prompt, mine, asked, later = [], [], [], []
    for d in (0, 2, 1, 3):
        tx = (x + d) % 4
        r, j = tx // 2, tx % 2
        copy = local if d == 0 else functools.partial(remote, dev=xdev(d))
        for which, ref in ((0, pkeys), (1, pvalues)):
            prompt.append(copy(ref.at[:, hd(j)], kv.at[y, grp, x, which]))
        (asked if d else mine).append(copy(queries.at[r, :, wide(j)], q_ref.at[x]))
        for which, ref in ((0, keys), (1, values)):
            (later if d else mine).append(copy(ref.at[r, :, hd(j)], kv.at[y, 2, x, which]))
        (later if d else mine).append(copy(gout.at[r, :, wide(j)], g_ref.at[x]))
    later = later[0::3] + later[1::3] + later[2::3]

    up, down = (y + 1) % 4, (y + 3) % 4

    def near(part):
        return [remote(kv.at[y, part], kv.at[y, part], ydev(d)) for d in (1, 3)]

    def far(part):
        low, high = pl.ds(0, 2), pl.ds(2, 2)
        return [
            remote(kv.at[up, part, low], kv.at[up, part, low], ydev(3)),
            remote(kv.at[down, part, high], kv.at[down, part, high], ydev(1)),
        ]

    def across(d):
        sy = (y - d) % 4
        return [remote(kv.at[sy, grp], kv.at[sy, grp], xdev(0, 1))]

    near_prompt, near_resp, far_prompt, far_resp = near(grp), near(2), far(grp), far(2)
    swap = {d: across(d) for d in range(4)}

    def start(copies):
        for copy in copies:
            copy.start()

    def wait(copies):
        for copy in copies:
            copy.wait()

    start(prompt + mine + asked)
    wait(prompt)
    start(near_prompt + swap[0])
    wait(mine + asked)
    start(later)

    OWN, OTHER = 0, 1
    uses = [(0, OWN), (0, OTHER), (1, OWN), (3, OWN), (1, OTHER), (2, OWN), (3, OTHER), (2, OTHER)]

    def half(kind):
        return (grp + kind) % 2

    def place(p):
        d, kind = uses[p]
        sy = (y - d) % 4
        for b in range(4):
            rs = slice(p * CH + b * T, p * CH + (b + 1) * T)
            ka[rs, :T] = kv[sy, half(kind), b, 0]
            ka[rs, T:] = kv[sy, half(kind), b, 0]
            va[rs, :T] = kv[sy, half(kind), b, 1]
            va[rs, T:] = jnp.ones((T, T), BF)

    def place_response():
        for sy in range(4):
            for i in range(4):
                rs = slice(4096 + i * CH + sy * T, 4096 + i * CH + (sy + 1) * T)
                ka[rs, :T] = kv[sy, 2, i, 0]
                ka[rs, T:] = kv[sy, 2, i, 0]
                va[rs, :T] = kv[sy, 2, i, 1]
                va[rs, T:] = jnp.ones((T, T), BF)

    def slot(c, i):
        n = c - PC
        if isinstance(c, int) and n >= 0:
            return 32 + 4 * n - (n * (n - 1)) // 2 + i - n
        return 4 * c + i

    def chunk_rows(c):
        return slice(c * CH, (c + 1) * CH) if isinstance(c, int) else pl.ds(mult(c * CH, CH), CH)

    def fold(s):
        return functools.reduce(jnp.maximum, [s[:, k * T:(k + 1) * T] for k in range(CH // T)])

    lane = lax.broadcasted_iota(jnp.int32, (R, T), 1)

    def prepare(i, _):
        for h in range(HEADS):
            rs = slice(h * T, (h + 1) * T)
            qs = q_ref[i, :, rs].astype(F32) * c2
            hi = qs.astype(BF)
            qa[i, rs, :T] = hi
            qa[i, rs, T:] = (qs - hi.astype(F32)).astype(BF)
        acc[i] = jnp.zeros((R, 2 * T), F32)
        mrun[i] = jnp.full((R, T), -jnp.inf, F32)
        stat[i] = jnp.zeros((R, T), F32)
        return 0

    def scores(i, c, slot):
        s = dot(qa[i], ka[chunk_rows(c), :], NT)
        s_ref[slot] = s
        return fold(s)

    def weigh(i, chunks, g, top):
        old = mrun[i]
        new = jnp.maximum(old, jnp.broadcast_to(jnp.max(top, 1, keepdims=True), (R, T)))
        mrun[i] = new
        stat[i] = jnp.where(lane == g, new, stat[i])
        fade = jnp.exp2(old - new)
        acc[i] *= jnp.concatenate([fade, fade], 1)
        for c, buf in chunks:
            mm = mrun[i]
            s = s_ref[buf]
            e = jnp.concatenate(
                [jnp.exp2(s[:, k * T:(k + 1) * T] - mm) for k in range(CH // T)], 1
            ).astype(BF)
            e_ref[slot(c, i)] = e
            acc[i] += dot(e, va[chunk_rows(c), :], NN)

    def prefix_group(g):
        for i in range(4):
            chunks = [(2 * g + n, (i % 2) * 2 + n) for n in range(2)]
            top = functools.reduce(jnp.maximum, [scores(i, c, buf) for c, buf in chunks])
            weigh(i, chunks, g, top)

    def response_tile(i):
        tops = [scores(i, PC + n, n) for n in range(i)]
        s = dot(qa[i], ka[chunk_rows(PC + i), :], NT)
        col = lax.broadcasted_iota(jnp.int32, (T, CH), 1)
        row = lax.broadcasted_iota(jnp.int32, (T, CH), 0) + y * T
        seen = col <= row
        s = jnp.concatenate(
            [jnp.where(seen, s[h * T:(h + 1) * T], -jnp.inf) for h in range(HEADS)], 0
        )
        s_ref[i] = s
        tops.append(fold(s))
        weigh(i, [(PC + n, n) for n in range(i + 1)], 4, functools.reduce(jnp.maximum, tops))
        stat[i] = jnp.exp2(stat[i] - mrun[i])
        pos = lax.broadcasted_iota(jnp.int32, (T, T), 0) + (i * CH + y * T)
        live = pos < lens_ref[resp]
        part = lax.broadcasted_iota(jnp.int32, (T, T), 1)
        for h in range(HEADS):
            rs = slice(h * T, (h + 1) * T)
            inv = 1.0 / acc[i, rs, T:]
            o = jnp.where(live, acc[i, rs, :T] * inv, 0.0).astype(BF)
            g = jnp.where(live, g_ref[i, :, rs].astype(F32), 0.0)
            g_ref[i, :, rs] = o
            d0 = -jnp.sum(g * o.astype(F32), 1, keepdims=True)
            d1 = d0.astype(BF).astype(F32)
            d2 = (d0 - d1).astype(BF).astype(F32)
            d3 = d0 - d1 - d2
            qa[i, rs, :T] = g.astype(BF)
            qa[i, rs, T:] = jnp.where(
                part == 0, d1, jnp.where(part == 1, d2, jnp.where(part == 2, d3, 0.0))
            ).astype(BF)
            gt[0, i, :, rs] = (q_ref[i, :, rs].astype(F32) * (inv * scale)).astype(BF).T
            gt[1, i, :, rs] = (g * inv).astype(BF).T
            turned[i, :, rs] = stat[i, rs, :].T[:8]
            acc[i, rs, T:] = inv * scale
        acc[i, :, :T] = jnp.zeros((R, T), F32)

    lax.fori_loop(0, 4, prepare, 0)

    def group(g, _):
        @pl.when(g == 0)
        def _():
            wait(near_prompt + swap[0])
            start(swap[1] + far_prompt)
            place(0)
            place(1)

        @pl.when(g == 1)
        def _():
            wait(later)
            start(near_resp)
            wait(swap[1])
            start(swap[3])
            place(2)
            place(3)

        @pl.when(g == 2)
        def _():
            wait(far_prompt)
            start(swap[2])
            wait(near_resp)
            start(far_resp)
            place(4)
            place(5)

        @pl.when(g == 3)
        def _():
            wait(swap[3] + swap[2])
            place(6)
            place(7)

        prefix_group(g)
        return 0

    lax.fori_loop(0, 4, group, 0)
    wait(far_resp)
    place_response()
    for i in range(4):
        response_tile(i)

    homes = []
    for d in range(4):
        tx = (x + d) % 4
        copy = local if d == 0 else functools.partial(remote, dev=xdev(d))
        homes.append(copy(g_ref.at[tx], attended.at[resp, :, wide(kvh)]))
    for copy in homes:
        copy.start()

    def scaled(g):
        for i in range(4):
            f = turned[i, pl.ds(g, 1), :]
            for w in range(2):
                gs[w, :, i * R:(i + 1) * R] = (gt[w, i].astype(F32) * f).astype(BF)

    def rows_part(i, c, g):
        kk = chunk_rows(c)
        dp = dot(qa[i], va[kk, :], NT)
        ds = (e_ref[slot(c, i)].astype(F32) * dp).astype(BF)
        ds_ref[i] = ds
        f = jnp.sum(jnp.where(lane == g, stat[i], 0.0), 1, keepdims=True)
        acc[i, :, :T] += f * dot(ds, ka[kk, :T], NN)

    def keys_part(c, first):
        n = (4 - first) * R
        base = slot(c, first)
        ds = ds_ref[first:].reshape(n, CH)
        e = e_ref[pl.ds(base, 4 - first)].reshape(n, CH)
        dk = dot(gs[0, :, first * R:], ds, NN)
        dv = dot(gs[1, :, first * R:], e, NN)
        return dk.T.astype(BF), dv.T.astype(BF)

    def all_rows(c, first, g):
        for i in range(first, 4):
            rows_part(i, c, g)

    scaled(4)
    for i in range(4):
        all_rows(PC + i, i, 4)
        for w, val in enumerate(keys_part(PC + i, i)):
            for b in range(4):
                kv[b, 2, i, w] = val[b * T:(b + 1) * T]

    def send_back(d, part):
        ty = (y + d) % 4
        return remote(kv.at[ty, part], rbuf.at[d - 1, part], ydev(d))

    def total(part, extra=None):
        def block(b, _):
            for w in range(2):
                acc4 = kv[y, part, b, w].astype(F32)
                for d in range(3):
                    acc4 = acc4 + rbuf[d, part, b, w].astype(F32)
                if extra is not None:
                    acc4 = acc4 + extra[b, w].astype(F32)
                kv[y, part, b, w] = acc4.astype(BF)
            return 0

        lax.fori_loop(0, 4, block, 0)

    hops = (2, 1, 3, 0)
    yback = {part: [send_back(d, half(part) if part < 2 else 2) for d in (2, 1, 3)] for part in (2, OTHER, OWN)}
    crossing = [remote(kv.at[y, half(OTHER)], zbuf, xdev(0, 1))]
    kept, asks = [], []
    for e in (2, 1, 3, 0):
        tx = (x + e) % 4
        copy = local if e == 0 else functools.partial(remote, dev=xdev(e))
        asks.append(copy(q_ref.at[tx], query_grad.at[resp, :, wide(kvh)]))
        for w, out in ((0, key_grad), (1, value_grad)):
            kept.append(copy(kv.at[y, 2, tx, w], out.at[resp, :, hd(kvh)]))
    start(yback[2])

    def put(p, ty, part):
        for w, val in enumerate(keys_part(p, 0)):
            for b in range(4):
                kv[ty, part, b, w] = val[b * T:(b + 1) * T]

    spots = [uses.index(((4 - d) % 4, kind)) for kind in (OTHER, OWN) for d in hops]

    def pick(n, table):
        return functools.reduce(lambda v, k: jnp.where(n == k, table[k], v), range(1, len(table)), table[0])

    def prompt_chunk(n, _):
        p = pick(n, spots)
        ty = (y + pick(n, hops * 2)) % 4
        part = half(jnp.where(n < 4, OTHER, OWN))
        scaled(p // 2)
        for i in range(4):
            rows_part(i, p, p // 2)
        put(p, ty, part)
        for k in range(7):
            if k != 3:
                @pl.when(n == k)
                def _():
                    yback[OTHER if k < 4 else OWN][k % 4].start()

        @pl.when(n == 2)
        def _():
            wait(yback[2])
            total(2)
            start(kept)

        @pl.when(n == 4)
        def _():
            wait(yback[OTHER])
            total(half(OTHER))
            start(crossing)

        return 0

    lax.fori_loop(0, 7, prompt_chunk, 0)
    scaled(spots[7] // 2)
    for i in range(4):
        rows_part(i, spots[7], spots[7] // 2)
    for i in range(4):
        for h in range(HEADS):
            rs = slice(h * T, (h + 1) * T)
            q_ref[i, :, rs] = (acc[i, rs, :T] * acc[i, rs, T:]).astype(BF)
    start(asks)
    put(spots[7], y, grp)
    wait(crossing + yback[OWN])
    total(grp, zbuf)
    tail = [remote(kv.at[y, grp, (x + e) % 4], pbuf.at[x], xdev(e)) for e in (2, 1, 3)]
    start(tail)
    pbuf[x] = kv[y, grp, x]
    wait(tail)
    for j in range(2):
        for w, out in ((0, pk_grad), (1, pv_grad)):
            out[:, j * T:(j + 1) * T] = (pbuf[j, w].astype(F32) + pbuf[2 + j, w].astype(F32)).astype(BF)
    wait(homes + kept + asks)
    assert counter[0] <= N_SEM and counter[1] <= N_SEM


def settle(*refs):
    n = len(refs) // 3
    arrived, left = refs[3 * n:]
    loads = [pltpu.make_async_copy(refs[k], refs[2 * n + k], arrived.at[k]) for k in range(n)]
    stores = [pltpu.make_async_copy(refs[2 * n + k], refs[n + k], left.at[k]) for k in range(n)]
    for copy in loads:
        copy.start()
    for load, store in zip(loads, stores):
        load.wait()
        store.start()
    for copy in stores:
        copy.wait()


def shards(queries, keys, values, prefix_keys, shared_prompt_values, lengths, grad_out):
    like = lambda a: jax.ShapeDtypeStruct(a.shape, BF)
    hbm = pl.BlockSpec(memory_space=pl.ANY)
    vmem = pl.BlockSpec(memory_space=pltpu.VMEM)
    V = pltpu.VMEM
    shapes = [like(queries), like(queries), like(keys), like(keys), like(prefix_keys), like(prefix_keys)]
    made = pl.pallas_call(
        kernel,
        out_shape=shapes,
        in_specs=[pl.BlockSpec(memory_space=pltpu.SMEM)] + [hbm] * 6,
        out_specs=[hbm] * 4 + [vmem] * 2,
        scratch_shapes=[
            V((4, T, R), BF), V((4, T, R), BF), V((4, 3, 4, 2, T, T), BF), V((3, 3, 4, 2, T, T), BF),
            V((4, 2, T, T), BF), V((4, 2, T, T), BF),
            V((6144, 256), BF), V((6144, 256), BF), V((4, R, 256), BF),
            V((2, 4, T, R), BF), V((2, T, 4 * R), BF), V((4, R, CH), F32), V((4, R, CH), BF), V((42, R, CH), BF),
            V((4, R, T), F32), V((4, R, T), F32), V((4, 8, R), F32), V((4, R, 256), F32),
            pltpu.SemaphoreType.DMA((N_SEM,)), pltpu.SemaphoreType.DMA((N_SEM,)),
            pltpu.SemaphoreType.DMA((N_SEM,)),
        ],
        compiler_params=pltpu.CompilerParams(
            collective_id=0, has_side_effects=True, vmem_limit_bytes=64 * 1024 * 1024
        ),
        name="attention",
    )(lengths, queries, keys, values, prefix_keys, shared_prompt_values, grad_out)
    return pl.pallas_call(
        settle,
        out_shape=shapes,
        in_specs=[hbm] * 6,
        out_specs=[hbm] * 6,
        scratch_shapes=[V(a.shape, BF) for a in shapes] + [pltpu.SemaphoreType.DMA((6,))] * 2,
        name="settle",
    )(*made)


def solution(mesh):
    acts, prompt = P("grp", "ctx", "head"), P(("grp", "ctx"), "head")
    return jax.shard_map(
        shards,
        mesh=mesh,
        in_specs=(acts, acts, acts, prompt, prompt, P("grp"), acts),
        out_specs=(acts, acts, acts, acts, prompt, prompt),
        check_vma=False,
    )
```

```python
import functools
import math

import jax
import jax.numpy as jnp
from jax import lax
from jax.experimental import pallas as pl
from jax.experimental.pallas import tpu as pltpu
from jax.sharding import PartitionSpec as P

MESH = pl.DeviceIdType.MESH
F32, BF = jnp.float32, jnp.bfloat16
T = 128
CH = 512
HEADS = 5
R = HEADS * T
PC = 8
NT = (((1,), (1,)), ((), ()))
NN = (((1,), (0,)), ((), ()))
dot = functools.partial(lax.dot_general, preferred_element_type=F32)
N_SEM = 64


def mult(v, n):
    return pl.multiple_of(v, n)


def kernel(
    lens_ref, queries, keys, values, pkeys, pvalues, gout,
    attended, query_grad, key_grad, value_grad, pk_grad, pv_grad,
    q_ref, g_ref, kv, rbuf, zbuf, pbuf,
    ka, va, qa, gt, gs, s_ref, ds_ref, e_ref, mrun, stat, turned, acc,
    send, recv, lsem,
):
    grp, ctx, head = lax.axis_index("grp"), lax.axis_index("ctx"), lax.axis_index("head")
    x, y = ctx // 4, ctx % 4
    resp, kvh = x // 2, x % 2
    c2 = 1.4426950408889634 / math.sqrt(T)
    scale = 1.0 / math.sqrt(T)

    def xdev(d, other=0):
        return ((grp + other) % 2, ((x + d) % 4) * 4 + y, head)

    def ydev(d):
        return (grp, x * 4 + (y + d) % 4, head)

    counter = [0, 0]

    def remote(src, dst, dev):
        k = counter[0]
        counter[0] += 1
        return pltpu.make_async_remote_copy(
            src_ref=src, dst_ref=dst, send_sem=send.at[k], recv_sem=recv.at[k],
            device_id=dev, device_id_type=MESH,
        )

    def local(src, dst):
        k = counter[1]
        counter[1] += 1
        return pltpu.make_async_copy(src, dst, lsem.at[k])

    partners = [xdev(d) for d in (1, 2, 3)] + [ydev(d) for d in (1, 2, 3)] + [xdev(0, 1)]
    barrier = pltpu.get_barrier_semaphore()
    for dev in partners:
        pl.semaphore_signal(barrier, inc=1, device_id=dev, device_id_type=MESH)
    pl.semaphore_wait(barrier, len(partners))

    def hd(j):
        return pl.ds(mult(j * T, T), T)

    def wide(j):
        return pl.ds(mult(j * R, T), R)

    prompt, mine, asked, given, graded = [], [], [], [], []
    for d in (0, 2, 1, 3):
        tx = (x + d) % 4
        r, j = tx // 2, tx % 2
        copy = local if d == 0 else functools.partial(remote, dev=xdev(d))
        for which, ref in ((0, pkeys), (1, pvalues)):
            prompt.append(copy(ref.at[:, hd(j)], kv.at[y, grp, x, which]))
        (asked if d else mine).append(copy(queries.at[r, :, wide(j)], q_ref.at[x]))
        for which, ref in ((0, keys), (1, values)):
            given.append(copy(ref.at[r, :, hd(j)], kv.at[y, 2, x, which]))
        (graded if d else mine).append(copy(gout.at[r, :, wide(j)], g_ref.at[x]))

    up, down = (y + 1) % 4, (y + 3) % 4

    def near(part):
        return [remote(kv.at[y, part], kv.at[y, part], ydev(d)) for d in (1, 3)]

    def far(part):
        low, high = pl.ds(0, 2), pl.ds(2, 2)
        return [
            remote(kv.at[up, part, low], kv.at[up, part, low], ydev(3)),
            remote(kv.at[down, part, high], kv.at[down, part, high], ydev(1)),
        ]

    def across(d):
        sy = (y - d) % 4
        return [remote(kv.at[sy, grp], kv.at[sy, grp], xdev(0, 1))]

    near_prompt, near_resp, far_prompt, far_resp = near(grp), near(2), far(grp), far(2)
    swap = {d: across(d) for d in range(4)}

    def start(copies):
        for copy in copies:
            copy.start()

    def wait(copies):
        for copy in copies:
            copy.wait()

    start(prompt + given + mine)
    wait(prompt)
    start(near_prompt + swap[0] + asked)
    wait(given + mine + asked)
    start(graded)

    OWN, OTHER = 0, 1
    uses = [(0, OWN), (0, OTHER), (1, OWN), (3, OWN), (1, OTHER), (2, OWN), (3, OTHER), (2, OTHER)]

    def half(kind):
        return (grp + kind) % 2

    def place(p):
        d, kind = uses[p]
        sy = (y - d) % 4
        for b in range(4):
            rs = slice(p * CH + b * T, p * CH + (b + 1) * T)
            ka[rs, :T] = kv[sy, half(kind), b, 0]
            ka[rs, T:] = kv[sy, half(kind), b, 0]
            va[rs, :T] = kv[sy, half(kind), b, 1]
            va[rs, T:] = jnp.ones((T, T), BF)

    def place_response():
        for sy in range(4):
            for i in range(4):
                rs = slice(4096 + i * CH + sy * T, 4096 + i * CH + (sy + 1) * T)
                ka[rs, :T] = kv[sy, 2, i, 0]
                ka[rs, T:] = kv[sy, 2, i, 0]
                va[rs, :T] = kv[sy, 2, i, 1]
                va[rs, T:] = jnp.ones((T, T), BF)

    def slot(c, i):
        n = c - PC
        if isinstance(c, int) and n >= 0:
            return 32 + 4 * n - (n * (n - 1)) // 2 + i - n
        return 4 * c + i

    def chunk_rows(c):
        return slice(c * CH, (c + 1) * CH) if isinstance(c, int) else pl.ds(mult(c * CH, CH), CH)

    def fold(s):
        return functools.reduce(jnp.maximum, [s[:, k * T:(k + 1) * T] for k in range(CH // T)])

    lane = lax.broadcasted_iota(jnp.int32, (R, T), 1)

    def prepare(i, _):
        for h in range(HEADS):
            rs = slice(h * T, (h + 1) * T)
            qs = q_ref[i, :, rs].astype(F32) * c2
            hi = qs.astype(BF)
            qa[i, rs, :T] = hi
            qa[i, rs, T:] = (qs - hi.astype(F32)).astype(BF)
        acc[i] = jnp.zeros((R, 2 * T), F32)
        mrun[i] = jnp.full((R, T), -jnp.inf, F32)
        stat[i] = jnp.zeros((R, T), F32)
        return 0

    def scores(i, c, slot):
        s = dot(qa[i], ka[chunk_rows(c), :], NT)
        s_ref[slot] = s
        return fold(s)

    def weigh(i, chunks, g, top):
        old = mrun[i]
        new = jnp.maximum(old, jnp.broadcast_to(jnp.max(top, 1, keepdims=True), (R, T)))
        mrun[i] = new
        stat[i] = jnp.where(lane == g, new, stat[i])
        fade = jnp.exp2(old - new)
        acc[i] *= jnp.concatenate([fade, fade], 1)
        for c, buf in chunks:
            mm = mrun[i]
            s = s_ref[buf]
            e = jnp.concatenate(
                [jnp.exp2(s[:, k * T:(k + 1) * T] - mm) for k in range(CH // T)], 1
            ).astype(BF)
            e_ref[slot(c, i)] = e
            acc[i] += dot(e, va[chunk_rows(c), :], NN)

    def prefix_group(g):
        for i in range(4):
            chunks = [(2 * g + n, (i % 2) * 2 + n) for n in range(2)]
            top = functools.reduce(jnp.maximum, [scores(i, c, buf) for c, buf in chunks])
            weigh(i, chunks, g + g // 3, top)

    def response_tile(i):
        tops = [scores(i, PC + n, n) for n in range(i)]
        s = dot(qa[i], ka[chunk_rows(PC + i), :], NT)
        col = lax.broadcasted_iota(jnp.int32, (T, CH), 1)
        row = lax.broadcasted_iota(jnp.int32, (T, CH), 0) + y * T
        seen = col <= row
        s = jnp.concatenate(
            [jnp.where(seen, s[h * T:(h + 1) * T], -jnp.inf) for h in range(HEADS)], 0
        )
        s_ref[i] = s
        tops.append(fold(s))
        weigh(i, [(PC + n, n) for n in range(i + 1)], 3, functools.reduce(jnp.maximum, tops))

    def conclude(i):
        stat[i] = jnp.exp2(stat[i] - mrun[i])
        pos = lax.broadcasted_iota(jnp.int32, (T, T), 0) + (i * CH + y * T)
        live = pos < lens_ref[resp]
        part = lax.broadcasted_iota(jnp.int32, (T, T), 1)
        for h in range(HEADS):
            rs = slice(h * T, (h + 1) * T)
            inv = 1.0 / acc[i, rs, T:]
            o = jnp.where(live, acc[i, rs, :T] * inv, 0.0).astype(BF)
            g = jnp.where(live, g_ref[i, :, rs].astype(F32), 0.0)
            g_ref[i, :, rs] = o
            d0 = -jnp.sum(g * o.astype(F32), 1, keepdims=True)
            d1 = d0.astype(BF).astype(F32)
            d2 = (d0 - d1).astype(BF).astype(F32)
            d3 = d0 - d1 - d2
            qa[i, rs, :T] = g.astype(BF)
            qa[i, rs, T:] = jnp.where(
                part == 0, d1, jnp.where(part == 1, d2, jnp.where(part == 2, d3, 0.0))
            ).astype(BF)
            gt[0, i, :, rs] = (q_ref[i, :, rs].astype(F32) * (inv * scale)).astype(BF).T
            gt[1, i, :, rs] = (g * inv).astype(BF).T
            turned[i, :, rs] = stat[i, rs, :].T[:8]
            acc[i, rs, T:] = inv * scale
        acc[i, :, :T] = jnp.zeros((R, T), F32)

    lax.fori_loop(0, 4, prepare, 0)

    def group(g, _):
        @pl.when(g == 0)
        def _():
            wait(near_prompt + swap[0])
            start(swap[1] + far_prompt)
            place(0)
            place(1)

        @pl.when(g == 1)
        def _():
            start(near_resp + swap[3])
            place(2)
            place(3)

        @pl.when(g == 2)
        def _():
            wait(far_prompt)
            start(swap[2])
            wait(near_resp + swap[1])
            start(far_resp)
            place(4)
            place(5)

        @pl.when(g == 3)
        def _():
            wait(far_resp)
            place_response()
            for i in range(4):
                response_tile(i)
            wait(swap[3] + swap[2])
            place(6)
            place(7)

        prefix_group(g)
        return 0

    lax.fori_loop(0, 4, group, 0)
    wait(graded)
    for i in range(4):
        conclude(i)

    homes = []
    for d in range(4):
        tx = (x + d) % 4
        copy = local if d == 0 else functools.partial(remote, dev=xdev(d))
        homes.append(copy(g_ref.at[tx], attended.at[resp, :, wide(kvh)]))
    for copy in homes:
        copy.start()

    def scaled(g):
        for i in range(4):
            f = turned[i, pl.ds(g, 1), :]
            for w in range(2):
                gs[w, :, i * R:(i + 1) * R] = (gt[w, i].astype(F32) * f).astype(BF)

    def rows_part(i, c, g):
        kk = chunk_rows(c)
        dp = dot(qa[i], va[kk, :], NT)
        ds = (e_ref[slot(c, i)].astype(F32) * dp).astype(BF)
        ds_ref[i] = ds
        f = jnp.sum(jnp.where(lane == g, stat[i], 0.0), 1, keepdims=True)
        acc[i, :, :T] += f * dot(ds, ka[kk, :T], NN)

    def keys_part(c, first):
        n = (4 - first) * R
        base = slot(c, first)
        ds = ds_ref[first:].reshape(n, CH)
        e = e_ref[pl.ds(base, 4 - first)].reshape(n, CH)
        dk = dot(gs[0, :, first * R:], ds, NN)
        dv = dot(gs[1, :, first * R:], e, NN)
        return dk.T.astype(BF), dv.T.astype(BF)

    def all_rows(c, first, g):
        for i in range(first, 4):
            rows_part(i, c, g)

    scaled(3)
    for i in range(4):
        all_rows(PC + i, i, 3)
        for w, val in enumerate(keys_part(PC + i, i)):
            for b in range(4):
                kv[b, 2, i, w] = val[b * T:(b + 1) * T]

    def send_back(d, part, place):
        ty = (y + d) % 4
        return remote(kv.at[ty, part], rbuf.at[d - 1, place], ydev(d))

    def total(part, place):
        def block(b, _):
            for w in range(2):
                acc4 = kv[y, part, b, w].astype(F32)
                for d in range(3):
                    acc4 = acc4 + rbuf[d, place, b, w].astype(F32)
                kv[y, part, b, w] = acc4.astype(BF)
            return 0

        lax.fori_loop(0, 4, block, 0)

    def join(ty):
        for b in range(4):
            for w in range(2):
                kv[ty, grp, b, w] = (kv[ty, grp, b, w].astype(F32) + zbuf[ty, b, w].astype(F32)).astype(BF)

    hops = (2, 1, 3, 0)
    back_resp = [send_back(d, 2, 0) for d in (2, 1, 3)]
    back_prompt = [send_back(d, grp, 1) for d in (2, 1, 3)]
    crossing = []
    for d in hops:
        ty = (y + d) % 4
        crossing.append(remote(kv.at[ty, half(OTHER)], zbuf.at[ty], xdev(0, 1)))
    kept, asks = [], []
    for e in (2, 1, 3, 0):
        tx = (x + e) % 4
        copy = local if e == 0 else functools.partial(remote, dev=xdev(e))
        asks.append(copy(q_ref.at[tx], query_grad.at[resp, :, wide(kvh)]))
        for w, out in ((0, key_grad), (1, value_grad)):
            kept.append(copy(kv.at[y, 2, tx, w], out.at[resp, :, hd(kvh)]))
    start(back_resp)

    def put(p, ty, part):
        for w, val in enumerate(keys_part(p, 0)):
            for b in range(4):
                kv[ty, part, b, w] = val[b * T:(b + 1) * T]

    spots = [uses.index(((4 - d) % 4, kind)) for kind in (OTHER, OWN) for d in hops]

    def pick(n, table):
        return functools.reduce(lambda v, k: jnp.where(n == k, table[k], v), range(1, len(table)), table[0])

    def prompt_chunk(n, _):
        p = pick(n, spots)
        ty = (y + pick(n, hops * 2)) % 4
        part = half(jnp.where(n < 4, OTHER, OWN))
        g = p // 2 + p // 6
        scaled(g)
        for i in range(4):
            rows_part(i, p, g)
        put(p, ty, part)
        for k in range(4):
            @pl.when(n == k)
            def _():
                crossing[k].start()

        for k in range(3):
            @pl.when(n == 4 + k)
            def _():
                crossing[k].wait()
                join(ty)
                back_prompt[k].start()

        @pl.when(n == 3)
        def _():
            wait(back_resp)
            total(2, 0)
            start(kept)

        return 0

    lax.fori_loop(0, 7, prompt_chunk, 0)
    scaled(spots[7] // 2)
    for i in range(4):
        rows_part(i, spots[7], spots[7] // 2)
    for i in range(4):
        for h in range(HEADS):
            rs = slice(h * T, (h + 1) * T)
            q_ref[i, :, rs] = (acc[i, rs, :T] * acc[i, rs, T:]).astype(BF)
    start(asks)
    put(spots[7], y, grp)
    crossing[3].wait()
    join(y)
    wait(back_prompt)
    total(grp, 1)
    tail = [remote(kv.at[y, grp, (x + e) % 4], pbuf.at[x], xdev(e)) for e in (2, 1, 3)]
    start(tail)
    pbuf[x] = kv[y, grp, x]
    wait(tail)
    for j in range(2):
        for w, out in ((0, pk_grad), (1, pv_grad)):
            out[:, j * T:(j + 1) * T] = (pbuf[j, w].astype(F32) + pbuf[2 + j, w].astype(F32)).astype(BF)
    wait(homes + kept + asks)
    assert counter[0] <= N_SEM and counter[1] <= N_SEM


def settle(*refs):
    n = len(refs) // 3
    arrived, left = refs[3 * n:]
    loads = [pltpu.make_async_copy(refs[k], refs[2 * n + k], arrived.at[k]) for k in range(n)]
    stores = [pltpu.make_async_copy(refs[2 * n + k], refs[n + k], left.at[k]) for k in range(n)]
    for copy in loads:
        copy.start()
    for load, store in zip(loads, stores):
        load.wait()
        store.start()
    for copy in stores:
        copy.wait()


def shards(queries, keys, values, prefix_keys, shared_prompt_values, lengths, grad_out):
    like = lambda a: jax.ShapeDtypeStruct(a.shape, BF)
    hbm = pl.BlockSpec(memory_space=pl.ANY)
    vmem = pl.BlockSpec(memory_space=pltpu.VMEM)
    V = pltpu.VMEM
    shapes = [like(queries), like(queries), like(keys), like(keys), like(prefix_keys), like(prefix_keys)]
    made = pl.pallas_call(
        kernel,
        out_shape=shapes,
        in_specs=[pl.BlockSpec(memory_space=pltpu.SMEM)] + [hbm] * 6,
        out_specs=[hbm] * 4 + [vmem] * 2,
        scratch_shapes=[
            V((4, T, R), BF), V((4, T, R), BF), V((4, 3, 4, 2, T, T), BF), V((3, 2, 4, 2, T, T), BF),
            V((4, 4, 2, T, T), BF), V((4, 2, T, T), BF),
            V((6144, 256), BF), V((6144, 256), BF), V((4, R, 256), BF),
            V((2, 4, T, R), BF), V((2, T, 4 * R), BF), V((4, R, CH), F32), V((4, R, CH), BF), V((42, R, CH), BF),
            V((4, R, T), F32), V((4, R, T), F32), V((4, 8, R), F32), V((4, R, 256), F32),
            pltpu.SemaphoreType.DMA((N_SEM,)), pltpu.SemaphoreType.DMA((N_SEM,)),
            pltpu.SemaphoreType.DMA((N_SEM,)),
        ],
        compiler_params=pltpu.CompilerParams(
            collective_id=0, has_side_effects=True, vmem_limit_bytes=64 * 1024 * 1024
        ),
        name="attention",
    )(lengths, queries, keys, values, prefix_keys, shared_prompt_values, grad_out)
    return pl.pallas_call(
        settle,
        out_shape=shapes,
        in_specs=[hbm] * 6,
        out_specs=[hbm] * 6,
        scratch_shapes=[V(a.shape, BF) for a in shapes] + [pltpu.SemaphoreType.DMA((6,))] * 2,
        name="settle",
    )(*made)


def solution(mesh):
    acts, prompt = P("grp", "ctx", "head"), P(("grp", "ctx"), "head")
    return jax.shard_map(
        shards,
        mesh=mesh,
        in_specs=(acts, acts, acts, prompt, prompt, P("grp"), acts),
        out_specs=(acts, acts, acts, acts, prompt, prompt),
        check_vma=False,
    )
```

```python
import functools
import math

import jax
import jax.numpy as jnp
from jax import lax
from jax.experimental import pallas as pl
from jax.experimental.pallas import tpu as pltpu
from jax.sharding import PartitionSpec as P

MESH = pl.DeviceIdType.MESH
F32, BF = jnp.float32, jnp.bfloat16
T = 128
CH = 512
HEADS = 5
R = HEADS * T
PC = 8
NT = (((1,), (1,)), ((), ()))
NN = (((1,), (0,)), ((), ()))
dot = functools.partial(lax.dot_general, preferred_element_type=F32)
N_SEM = 64


def mult(v, n):
    return pl.multiple_of(v, n)


def kernel(
    lens_ref, queries, keys, values, pkeys, pvalues, gout,
    attended, query_grad, key_grad, value_grad, pk_grad, pv_grad,
    q_ref, g_ref, kv, rbuf, zbuf, pbuf,
    ka, va, qa, gt, gs, s_ref, ds_ref, e_ref, mrun, stat, turned, acc,
    send, recv, lsem,
):
    grp, ctx, head = lax.axis_index("grp"), lax.axis_index("ctx"), lax.axis_index("head")
    x, y = ctx // 4, ctx % 4
    resp, kvh = x // 2, x % 2
    c2 = 1.4426950408889634 / math.sqrt(T)
    scale = 1.0 / math.sqrt(T)

    def xdev(d, other=0):
        return ((grp + other) % 2, ((x + d) % 4) * 4 + y, head)

    def ydev(d):
        return (grp, x * 4 + (y + d) % 4, head)

    counter = [0, 0]

    def remote(src, dst, dev):
        k = counter[0]
        counter[0] += 1
        return pltpu.make_async_remote_copy(
            src_ref=src, dst_ref=dst, send_sem=send.at[k], recv_sem=recv.at[k],
            device_id=dev, device_id_type=MESH,
        )

    def local(src, dst):
        k = counter[1]
        counter[1] += 1
        return pltpu.make_async_copy(src, dst, lsem.at[k])

    partners = [xdev(d) for d in (1, 2, 3)] + [ydev(d) for d in (1, 2, 3)] + [xdev(0, 1)]
    barrier = pltpu.get_barrier_semaphore()
    for dev in partners:
        pl.semaphore_signal(barrier, inc=1, device_id=dev, device_id_type=MESH)
    pl.semaphore_wait(barrier, len(partners))

    def hd(j):
        return pl.ds(mult(j * T, T), T)

    def wide(j):
        return pl.ds(mult(j * R, T), R)

    prompt, mine, asked, given, graded = [], [], [], [], []
    for d in (0, 2, 1, 3):
        tx = (x + d) % 4
        r, j = tx // 2, tx % 2
        copy = local if d == 0 else functools.partial(remote, dev=xdev(d))
        for which, ref in ((0, pkeys), (1, pvalues)):
            prompt.append(copy(ref.at[:, hd(j)], kv.at[y, grp, x, which]))
        (asked if d else mine).append(copy(queries.at[r, :, wide(j)], q_ref.at[x]))
        for which, ref in ((0, keys), (1, values)):
            given.append(copy(ref.at[r, :, hd(j)], kv.at[y, 2, x, which]))
        (graded if d else mine).append(copy(gout.at[r, :, wide(j)], g_ref.at[x]))

    up, down = (y + 1) % 4, (y + 3) % 4

    def near(part):
        return [remote(kv.at[y, part], kv.at[y, part], ydev(d)) for d in (1, 3)]

    def far(part):
        low, high = pl.ds(0, 2), pl.ds(2, 2)
        return [
            remote(kv.at[up, part, low], kv.at[up, part, low], ydev(3)),
            remote(kv.at[down, part, high], kv.at[down, part, high], ydev(1)),
        ]

    def across(d):
        sy = (y - d) % 4
        return [remote(kv.at[sy, grp], kv.at[sy, grp], xdev(0, 1))]

    near_prompt, near_resp, far_prompt, far_resp = near(grp), near(2), far(grp), far(2)
    swap = {d: across(d) for d in range(4)}

    def start(copies):
        for copy in copies:
            copy.start()

    def wait(copies):
        for copy in copies:
            copy.wait()

    start(prompt + mine)
    wait(prompt)
    start(near_prompt + swap[0] + asked)
    wait(near_prompt)
    start(swap[1] + far_prompt)
    wait(mine + asked)
    start(given)

    OWN, OTHER = 0, 1
    uses = [(0, OWN), (0, OTHER), (1, OWN), (3, OWN), (1, OTHER), (2, OWN), (3, OTHER), (2, OTHER)]

    def half(kind):
        return (grp + kind) % 2

    def place(p):
        d, kind = uses[p]
        sy = (y - d) % 4
        for b in range(4):
            rs = slice(p * CH + b * T, p * CH + (b + 1) * T)
            ka[rs, :T] = kv[sy, half(kind), b, 0]
            ka[rs, T:] = kv[sy, half(kind), b, 0]
            va[rs, :T] = kv[sy, half(kind), b, 1]
            va[rs, T:] = jnp.ones((T, T), BF)

    def place_response():
        for sy in range(4):
            for i in range(4):
                rs = slice(4096 + i * CH + sy * T, 4096 + i * CH + (sy + 1) * T)
                ka[rs, :T] = kv[sy, 2, i, 0]
                ka[rs, T:] = kv[sy, 2, i, 0]
                va[rs, :T] = kv[sy, 2, i, 1]
                va[rs, T:] = jnp.ones((T, T), BF)

    def slot(c, i):
        n = c - PC
        if isinstance(c, int) and n >= 0:
            return 32 + 4 * n - (n * (n - 1)) // 2 + i - n
        return 4 * c + i

    def chunk_rows(c):
        return slice(c * CH, (c + 1) * CH) if isinstance(c, int) else pl.ds(mult(c * CH, CH), CH)

    def fold(s):
        return functools.reduce(jnp.maximum, [s[:, k * T:(k + 1) * T] for k in range(CH // T)])

    lane = lax.broadcasted_iota(jnp.int32, (R, T), 1)

    def prepare(i, _):
        for h in range(HEADS):
            rs = slice(h * T, (h + 1) * T)
            qs = q_ref[i, :, rs].astype(F32) * c2
            hi = qs.astype(BF)
            qa[i, rs, :T] = hi
            qa[i, rs, T:] = (qs - hi.astype(F32)).astype(BF)
        acc[i] = jnp.zeros((R, 2 * T), F32)
        mrun[i] = jnp.full((R, T), -jnp.inf, F32)
        stat[i] = jnp.zeros((R, T), F32)
        return 0

    def scores(i, c, slot):
        s = dot(qa[i], ka[chunk_rows(c), :], NT)
        s_ref[slot] = s
        return fold(s)

    def weigh(i, chunks, g, top):
        old = mrun[i]
        new = jnp.maximum(old, jnp.broadcast_to(jnp.max(top, 1, keepdims=True), (R, T)))
        mrun[i] = new
        stat[i] = jnp.where(lane == g, new, stat[i])
        fade = jnp.exp2(old - new)
        acc[i] *= jnp.concatenate([fade, fade], 1)
        for c, buf in chunks:
            mm = mrun[i]
            s = s_ref[buf]
            e = jnp.concatenate(
                [jnp.exp2(s[:, k * T:(k + 1) * T] - mm) for k in range(CH // T)], 1
            ).astype(BF)
            e_ref[slot(c, i)] = e
            acc[i] += dot(e, va[chunk_rows(c), :], NN)

    def prefix_group(g):
        for i in range(4):
            chunks = [(2 * g + n, (i % 2) * 2 + n) for n in range(2)]
            top = functools.reduce(jnp.maximum, [scores(i, c, buf) for c, buf in chunks])
            weigh(i, chunks, g + g // 3, top)

    def response_tile(i):
        tops = [scores(i, PC + n, n) for n in range(i)]
        s = dot(qa[i], ka[chunk_rows(PC + i), :], NT)
        col = lax.broadcasted_iota(jnp.int32, (T, CH), 1)
        row = lax.broadcasted_iota(jnp.int32, (T, CH), 0) + y * T
        seen = col <= row
        s = jnp.concatenate(
            [jnp.where(seen, s[h * T:(h + 1) * T], -jnp.inf) for h in range(HEADS)], 0
        )
        s_ref[i] = s
        tops.append(fold(s))
        weigh(i, [(PC + n, n) for n in range(i + 1)], 3, functools.reduce(jnp.maximum, tops))

    def conclude(i):
        stat[i] = jnp.exp2(stat[i] - mrun[i])
        pos = lax.broadcasted_iota(jnp.int32, (T, T), 0) + (i * CH + y * T)
        live = pos < lens_ref[resp]
        part = lax.broadcasted_iota(jnp.int32, (T, T), 1)
        for h in range(HEADS):
            rs = slice(h * T, (h + 1) * T)
            inv = 1.0 / acc[i, rs, T:]
            o = jnp.where(live, acc[i, rs, :T] * inv, 0.0).astype(BF)
            g = jnp.where(live, g_ref[i, :, rs].astype(F32), 0.0)
            g_ref[i, :, rs] = o
            d0 = -jnp.sum(g * o.astype(F32), 1, keepdims=True)
            d1 = d0.astype(BF).astype(F32)
            d2 = (d0 - d1).astype(BF).astype(F32)
            d3 = d0 - d1 - d2
            qa[i, rs, :T] = g.astype(BF)
            qa[i, rs, T:] = jnp.where(
                part == 0, d1, jnp.where(part == 1, d2, jnp.where(part == 2, d3, 0.0))
            ).astype(BF)
            gt[0, i, :, rs] = (q_ref[i, :, rs].astype(F32) * (inv * scale)).astype(BF).T
            gt[1, i, :, rs] = (g * inv).astype(BF).T
            turned[i, :, rs] = stat[i, rs, :].T[:8]
            acc[i, rs, T:] = inv * scale
        acc[i, :, :T] = jnp.zeros((R, T), F32)

    lax.fori_loop(0, 4, prepare, 0)

    def group(g, _):
        @pl.when(g == 0)
        def _():
            wait(swap[0])
            start(swap[3])
            place(0)
            place(1)

        @pl.when(g == 1)
        def _():
            wait(given)
            start(near_resp + graded)
            wait(far_prompt)
            start(swap[2])
            place(2)
            place(3)

        @pl.when(g == 2)
        def _():
            wait(near_resp)
            start(far_resp)
            wait(swap[1])
            place(4)
            place(5)

        @pl.when(g == 3)
        def _():
            wait(far_resp)
            place_response()
            for i in range(4):
                response_tile(i)
            wait(swap[3] + swap[2])
            place(6)
            place(7)

        prefix_group(g)
        return 0

    lax.fori_loop(0, 4, group, 0)
    wait(graded)
    for i in range(4):
        conclude(i)

    homes = []
    for d in range(4):
        tx = (x + d) % 4
        copy = local if d == 0 else functools.partial(remote, dev=xdev(d))
        homes.append(copy(g_ref.at[tx], attended.at[resp, :, wide(kvh)]))
    for copy in homes:
        copy.start()

    def scaled(g):
        for i in range(4):
            f = turned[i, pl.ds(g, 1), :]
            for w in range(2):
                gs[w, :, i * R:(i + 1) * R] = (gt[w, i].astype(F32) * f).astype(BF)

    def rows_part(i, c, g):
        kk = chunk_rows(c)
        dp = dot(qa[i], va[kk, :], NT)
        ds = (e_ref[slot(c, i)].astype(F32) * dp).astype(BF)
        ds_ref[i] = ds
        f = jnp.sum(jnp.where(lane == g, stat[i], 0.0), 1, keepdims=True)
        acc[i, :, :T] += f * dot(ds, ka[kk, :T], NN)

    def keys_part(c, first):
        n = (4 - first) * R
        base = slot(c, first)
        ds = ds_ref[first:].reshape(n, CH)
        e = e_ref[pl.ds(base, 4 - first)].reshape(n, CH)
        dk = dot(gs[0, :, first * R:], ds, NN)
        dv = dot(gs[1, :, first * R:], e, NN)
        return dk.T.astype(BF), dv.T.astype(BF)

    def all_rows(c, first, g):
        for i in range(first, 4):
            rows_part(i, c, g)

    def response_chunks():
        scaled(3)
        for i in range(4):
            all_rows(PC + i, i, 3)
            for w, val in enumerate(keys_part(PC + i, i)):
                for b in range(4):
                    kv[b, 2, i, w] = val[b * T:(b + 1) * T]

    def send_back(d, part, place):
        ty = (y + d) % 4
        return remote(kv.at[ty, part], rbuf.at[d - 1, place], ydev(d))

    def total(part, place):
        def block(b, _):
            for w in range(2):
                acc4 = kv[y, part, b, w].astype(F32)
                for d in range(3):
                    acc4 = acc4 + rbuf[d, place, b, w].astype(F32)
                kv[y, part, b, w] = acc4.astype(BF)
            return 0

        lax.fori_loop(0, 4, block, 0)

    def join(ty):
        for b in range(4):
            for w in range(2):
                kv[ty, grp, b, w] = (kv[ty, grp, b, w].astype(F32) + zbuf[ty, b, w].astype(F32)).astype(BF)

    hops = (2, 1, 3, 0)
    back_resp = [send_back(d, 2, 0) for d in (2, 1, 3)]
    back_prompt = [send_back(d, grp, 1) for d in (2, 1, 3)]
    crossing = []
    for d in hops:
        ty = (y + d) % 4
        crossing.append(remote(kv.at[ty, half(OTHER)], zbuf.at[ty], xdev(0, 1)))
    kept, asks = [], []
    for e in (2, 1, 3, 0):
        tx = (x + e) % 4
        copy = local if e == 0 else functools.partial(remote, dev=xdev(e))
        asks.append(copy(q_ref.at[tx], query_grad.at[resp, :, wide(kvh)]))
        for w, out in ((0, key_grad), (1, value_grad)):
            kept.append(copy(kv.at[y, 2, tx, w], out.at[resp, :, hd(kvh)]))

    def put(p, ty, part):
        for w, val in enumerate(keys_part(p, 0)):
            for b in range(4):
                kv[ty, part, b, w] = val[b * T:(b + 1) * T]

    spots = [uses.index(((4 - d) % 4, kind)) for kind in (OTHER, OWN) for d in hops]

    def pick(n, table):
        return functools.reduce(lambda v, k: jnp.where(n == k, table[k], v), range(1, len(table)), table[0])

    def prompt_chunk(n, _):
        p = pick(n, spots)
        ty = (y + pick(n, hops * 2)) % 4
        part = half(jnp.where(n < 4, OTHER, OWN))

        @pl.when(n == 1)
        def _():
            response_chunks()
            start(back_resp)

        g = p // 2 + p // 6
        scaled(g)
        for i in range(4):
            rows_part(i, p, g)
        put(p, ty, part)
        for k in range(4):
            @pl.when(n == k)
            def _():
                crossing[k].start()

        for k in range(3):
            @pl.when(n == 4 + k)
            def _():
                crossing[k].wait()
                join(ty)
                back_prompt[k].start()

        @pl.when(n == 5)
        def _():
            wait(back_resp)
            total(2, 0)
            start(kept)

        return 0

    lax.fori_loop(0, 7, prompt_chunk, 0)
    scaled(spots[7] // 2)
    for i in range(4):
        rows_part(i, spots[7], spots[7] // 2)
    for i in range(4):
        for h in range(HEADS):
            rs = slice(h * T, (h + 1) * T)
            q_ref[i, :, rs] = (acc[i, rs, :T] * acc[i, rs, T:]).astype(BF)
    start(asks)
    put(spots[7], y, grp)
    crossing[3].wait()
    join(y)
    wait(back_prompt)
    total(grp, 1)
    tail = [remote(kv.at[y, grp, (x + e) % 4], pbuf.at[x], xdev(e)) for e in (2, 1, 3)]
    start(tail)
    pbuf[x] = kv[y, grp, x]
    wait(tail)
    for j in range(2):
        for w, out in ((0, pk_grad), (1, pv_grad)):
            out[:, j * T:(j + 1) * T] = (pbuf[j, w].astype(F32) + pbuf[2 + j, w].astype(F32)).astype(BF)
    wait(homes + kept + asks)
    assert counter[0] <= N_SEM and counter[1] <= N_SEM


def settle(*refs):
    n = len(refs) // 3
    arrived, left = refs[3 * n:]
    loads = [pltpu.make_async_copy(refs[k], refs[2 * n + k], arrived.at[k]) for k in range(n)]
    stores = [pltpu.make_async_copy(refs[2 * n + k], refs[n + k], left.at[k]) for k in range(n)]
    for copy in loads:
        copy.start()
    for load, store in zip(loads, stores):
        load.wait()
        store.start()
    for copy in stores:
        copy.wait()


def shards(queries, keys, values, prefix_keys, shared_prompt_values, lengths, grad_out):
    like = lambda a: jax.ShapeDtypeStruct(a.shape, BF)
    hbm = pl.BlockSpec(memory_space=pl.ANY)
    vmem = pl.BlockSpec(memory_space=pltpu.VMEM)
    V = pltpu.VMEM
    shapes = [like(queries), like(queries), like(keys), like(keys), like(prefix_keys), like(prefix_keys)]
    made = pl.pallas_call(
        kernel,
        out_shape=shapes,
        in_specs=[pl.BlockSpec(memory_space=pltpu.SMEM)] + [hbm] * 6,
        out_specs=[hbm] * 4 + [vmem] * 2,
        scratch_shapes=[
            V((4, T, R), BF), V((4, T, R), BF), V((4, 3, 4, 2, T, T), BF), V((3, 2, 4, 2, T, T), BF),
            V((4, 4, 2, T, T), BF), V((4, 2, T, T), BF),
            V((6144, 256), BF), V((6144, 256), BF), V((4, R, 256), BF),
            V((2, 4, T, R), BF), V((2, T, 4 * R), BF), V((4, R, CH), F32), V((4, R, CH), BF), V((42, R, CH), BF),
            V((4, R, T), F32), V((4, R, T), F32), V((4, 8, R), F32), V((4, R, 256), F32),
            pltpu.SemaphoreType.DMA((N_SEM,)), pltpu.SemaphoreType.DMA((N_SEM,)),
            pltpu.SemaphoreType.DMA((N_SEM,)),
        ],
        compiler_params=pltpu.CompilerParams(
            collective_id=0, has_side_effects=True, vmem_limit_bytes=64 * 1024 * 1024
        ),
        name="attention",
    )(lengths, queries, keys, values, prefix_keys, shared_prompt_values, grad_out)
    return pl.pallas_call(
        settle,
        out_shape=shapes,
        in_specs=[hbm] * 6,
        out_specs=[hbm] * 6,
        scratch_shapes=[V(a.shape, BF) for a in shapes] + [pltpu.SemaphoreType.DMA((6,))] * 2,
        name="settle",
    )(*made)


def solution(mesh):
    acts, prompt = P("grp", "ctx", "head"), P(("grp", "ctx"), "head")
    return jax.shard_map(
        shards,
        mesh=mesh,
        in_specs=(acts, acts, acts, prompt, prompt, P("grp"), acts),
        out_specs=(acts, acts, acts, acts, prompt, prompt),
        check_vma=False,
    )
```

```python
import functools
import math

import jax
import jax.numpy as jnp
from jax import lax
from jax.experimental import pallas as pl
from jax.experimental.pallas import tpu as pltpu
from jax.sharding import PartitionSpec as P

MESH = pl.DeviceIdType.MESH
F32, BF = jnp.float32, jnp.bfloat16
T = 128
CH = 512
HEADS = 5
R = HEADS * T
PC = 8
NT = (((1,), (1,)), ((), ()))
NN = (((1,), (0,)), ((), ()))
dot = functools.partial(lax.dot_general, preferred_element_type=F32)
N_SEM = 64


def mult(v, n):
    return pl.multiple_of(v, n)


def kernel(
    lens_ref, queries, keys, values, pkeys, pvalues, gout,
    attended, query_grad, key_grad, value_grad, pk_grad, pv_grad,
    q_ref, g_ref, kv, rbuf, zbuf, pbuf,
    ka, va, qa, gt, gs, s_ref, ds_ref, e_ref, mrun, stat, turned, acc,
    send, recv, lsem,
):
    grp, ctx, head = lax.axis_index("grp"), lax.axis_index("ctx"), lax.axis_index("head")
    x, y = ctx // 4, ctx % 4
    resp, kvh = x // 2, x % 2
    c2 = 1.4426950408889634 / math.sqrt(T)
    scale = 1.0 / math.sqrt(T)

    def xdev(d, other=0):
        return ((grp + other) % 2, ((x + d) % 4) * 4 + y, head)

    def ydev(d):
        return (grp, x * 4 + (y + d) % 4, head)

    counter = [0, 0]

    def remote(src, dst, dev):
        k = counter[0]
        counter[0] += 1
        return pltpu.make_async_remote_copy(
            src_ref=src, dst_ref=dst, send_sem=send.at[k], recv_sem=recv.at[k],
            device_id=dev, device_id_type=MESH,
        )

    def local(src, dst):
        k = counter[1]
        counter[1] += 1
        return pltpu.make_async_copy(src, dst, lsem.at[k])

    partners = [xdev(d) for d in (1, 2, 3)] + [ydev(d) for d in (1, 2, 3)] + [xdev(0, 1)]
    barrier = pltpu.get_barrier_semaphore()
    for dev in partners:
        pl.semaphore_signal(barrier, inc=1, device_id=dev, device_id_type=MESH)
    pl.semaphore_wait(barrier, len(partners))

    def hd(j):
        return pl.ds(mult(j * T, T), T)

    def wide(j):
        return pl.ds(mult(j * R, T), R)

    prompt, mine, asked, given, graded = [], [], [], [], []
    for d in (0, 2, 1, 3):
        tx = (x + d) % 4
        r, j = tx // 2, tx % 2
        copy = local if d == 0 else functools.partial(remote, dev=xdev(d))
        for which, ref in ((0, pkeys), (1, pvalues)):
            prompt.append(copy(ref.at[:, hd(j)], kv.at[y, grp, x, which]))
        (asked if d else mine).append(copy(queries.at[r, :, wide(j)], q_ref.at[x]))
        for which, ref in ((0, keys), (1, values)):
            given.append(copy(ref.at[r, :, hd(j)], kv.at[y, 2, x, which]))
        (graded if d else mine).append(copy(gout.at[r, :, wide(j)], g_ref.at[x]))

    up, down = (y + 1) % 4, (y + 3) % 4

    def near(part):
        return [remote(kv.at[y, part], kv.at[y, part], ydev(d)) for d in (1, 3)]

    def far(part):
        low, high = pl.ds(0, 2), pl.ds(2, 2)
        return [
            remote(kv.at[up, part, low], kv.at[up, part, low], ydev(3)),
            remote(kv.at[down, part, high], kv.at[down, part, high], ydev(1)),
        ]

    def across(d):
        sy = (y - d) % 4
        return [remote(kv.at[sy, grp], kv.at[sy, grp], xdev(0, 1))]

    near_prompt, near_resp, far_prompt, far_resp = near(grp), near(2), far(grp), far(2)
    swap = {d: across(d) for d in range(4)}

    def start(copies):
        for copy in copies:
            copy.start()

    def wait(copies):
        for copy in copies:
            copy.wait()

    start(prompt + mine)
    wait(prompt)
    start(near_prompt + swap[0] + asked)
    wait(near_prompt)
    start(swap[1] + far_prompt)

    OWN, OTHER = 0, 1
    uses = [(0, OWN), (0, OTHER), (1, OWN), (3, OWN), (1, OTHER), (2, OWN), (3, OTHER), (2, OTHER)]

    def half(kind):
        return (grp + kind) % 2

    def place(p):
        d, kind = uses[p]
        sy = (y - d) % 4
        for b in range(4):
            rs = slice(p * CH + b * T, p * CH + (b + 1) * T)
            ka[rs, :T] = kv[sy, half(kind), b, 0]
            ka[rs, T:] = kv[sy, half(kind), b, 0]
            va[rs, :T] = kv[sy, half(kind), b, 1]
            va[rs, T:] = jnp.ones((T, T), BF)

    def place_response():
        for sy in range(4):
            for i in range(4):
                rs = slice(4096 + i * CH + sy * T, 4096 + i * CH + (sy + 1) * T)
                ka[rs, :T] = kv[sy, 2, i, 0]
                ka[rs, T:] = kv[sy, 2, i, 0]
                va[rs, :T] = kv[sy, 2, i, 1]
                va[rs, T:] = jnp.ones((T, T), BF)

    def slot(c, i):
        n = c - PC
        if isinstance(c, int) and n >= 0:
            return 32 + 4 * n - (n * (n - 1)) // 2 + i - n
        return 4 * c + i

    def chunk_rows(c):
        return slice(c * CH, (c + 1) * CH) if isinstance(c, int) else pl.ds(mult(c * CH, CH), CH)

    def fold(s):
        return functools.reduce(jnp.maximum, [s[:, k * T:(k + 1) * T] for k in range(CH // T)])

    lane = lax.broadcasted_iota(jnp.int32, (R, T), 1)

    def prepare(i, _):
        for h in range(HEADS):
            rs = slice(h * T, (h + 1) * T)
            qs = q_ref[i, :, rs].astype(F32) * c2
            hi = qs.astype(BF)
            qa[i, rs, :T] = hi
            qa[i, rs, T:] = (qs - hi.astype(F32)).astype(BF)
        return 0

    def clear(i, _):
        acc[i] = jnp.zeros((R, 2 * T), F32)
        mrun[i] = jnp.full((R, T), -jnp.inf, F32)
        stat[i] = jnp.zeros((R, T), F32)
        return 0

    def scores(i, c, slot):
        s = dot(qa[i], ka[chunk_rows(c), :], NT)
        s_ref[slot] = s
        return fold(s)

    def weigh(i, chunks, g, top):
        old = mrun[i]
        new = jnp.maximum(old, jnp.broadcast_to(jnp.max(top, 1, keepdims=True), (R, T)))
        mrun[i] = new
        stat[i] = jnp.where(lane == g, new, stat[i])
        fade = jnp.exp2(old - new)
        es = []
        for c, buf in chunks:
            s = s_ref[buf]
            e = jnp.concatenate(
                [jnp.exp2(s[:, k * T:(k + 1) * T] - new) for k in range(CH // T)], 1
            ).astype(BF)
            e_ref[slot(c, i)] = e
            es.append(e)
        first = chunks[0][0] * CH
        keys_in = pl.ds(first if isinstance(first, int) else mult(first, CH), CH * len(chunks))
        acc[i] = acc[i] * jnp.concatenate([fade, fade], 1) + dot(jnp.concatenate(es, 1), va[keys_in, :], NN)

    def prefix_group(g):
        for i in range(4):
            chunks = [(2 * g + n, (i % 2) * 2 + n) for n in range(2)]
            top = functools.reduce(jnp.maximum, [scores(i, c, buf) for c, buf in chunks])
            weigh(i, chunks, g + g // 3, top)

    def response_tile(i):
        tops = [scores(i, PC + n, n) for n in range(i)]
        s = dot(qa[i], ka[chunk_rows(PC + i), :], NT)
        col = lax.broadcasted_iota(jnp.int32, (T, CH), 1)
        row = lax.broadcasted_iota(jnp.int32, (T, CH), 0) + y * T
        seen = col <= row
        s = jnp.concatenate(
            [jnp.where(seen, s[h * T:(h + 1) * T], -jnp.inf) for h in range(HEADS)], 0
        )
        s_ref[i] = s
        tops.append(fold(s))
        weigh(i, [(PC + n, n) for n in range(i + 1)], 3, functools.reduce(jnp.maximum, tops))

    def conclude(i):
        stat[i] = jnp.exp2(stat[i] - mrun[i])
        pos = lax.broadcasted_iota(jnp.int32, (T, T), 0) + (i * CH + y * T)
        live = pos < lens_ref[resp]
        part = lax.broadcasted_iota(jnp.int32, (T, T), 1)
        for h in range(HEADS):
            rs = slice(h * T, (h + 1) * T)
            inv = 1.0 / acc[i, rs, T:]
            o = jnp.where(live, acc[i, rs, :T] * inv, 0.0).astype(BF)
            g = jnp.where(live, g_ref[i, :, rs].astype(F32), 0.0)
            g_ref[i, :, rs] = o
            d0 = -jnp.sum(g * o.astype(F32), 1, keepdims=True)
            d1 = d0.astype(BF).astype(F32)
            d2 = (d0 - d1).astype(BF).astype(F32)
            d3 = d0 - d1 - d2
            qa[i, rs, :T] = g.astype(BF)
            qa[i, rs, T:] = jnp.where(
                part == 0, d1, jnp.where(part == 1, d2, jnp.where(part == 2, d3, 0.0))
            ).astype(BF)
            gt[0, i, :, rs] = (q_ref[i, :, rs].astype(F32) * (inv * scale)).astype(BF).T
            gt[1, i, :, rs] = (g * inv).astype(BF).T
            turned[i, :, rs] = stat[i, rs, :].T[:8]
            acc[i, rs, T:] = inv * scale
        acc[i, :, :T] = jnp.zeros((R, T), F32)

    lax.fori_loop(0, 4, clear, 0)
    wait(mine + asked)
    start(given)
    lax.fori_loop(0, 4, prepare, 0)

    def group(g, _):
        @pl.when(g == 0)
        def _():
            wait(swap[0])
            start(swap[3])
            place(0)
            place(1)

        @pl.when(g == 1)
        def _():
            wait(given)
            start(near_resp + graded)
            wait(far_prompt)
            start(swap[2])
            place(2)
            place(3)

        @pl.when(g == 2)
        def _():
            wait(near_resp)
            start(far_resp)
            wait(swap[1])
            place(4)
            place(5)

        @pl.when(g == 3)
        def _():
            wait(far_resp)
            place_response()
            for i in range(4):
                response_tile(i)
            wait(swap[3] + swap[2])
            place(6)
            place(7)

        prefix_group(g)
        return 0

    lax.fori_loop(0, 4, group, 0)
    wait(graded)
    for i in range(4):
        conclude(i)

    homes = []
    for d in range(4):
        tx = (x + d) % 4
        copy = local if d == 0 else functools.partial(remote, dev=xdev(d))
        homes.append(copy(g_ref.at[tx], attended.at[resp, :, wide(kvh)]))
    for copy in homes:
        copy.start()

    def scaled(g):
        for i in range(4):
            f = turned[i, pl.ds(g, 1), :]
            for w in range(2):
                gs[w, :, i * R:(i + 1) * R] = (gt[w, i].astype(F32) * f).astype(BF)

    def rows_part(i, c, g):
        kk = chunk_rows(c)
        dp = dot(qa[i], va[kk, :], NT)
        ds = (e_ref[slot(c, i)].astype(F32) * dp).astype(BF)
        ds_ref[i] = ds
        f = jnp.sum(jnp.where(lane == g, stat[i], 0.0), 1, keepdims=True)
        acc[i, :, :T] += f * dot(ds, ka[kk, :T], NN)

    def keys_part(c, first):
        n = (4 - first) * R
        base = slot(c, first)
        ds = ds_ref[first:].reshape(n, CH)
        e = e_ref[pl.ds(base, 4 - first)].reshape(n, CH)
        dk = dot(gs[0, :, first * R:], ds, NN)
        dv = dot(gs[1, :, first * R:], e, NN)
        return dk.T.astype(BF), dv.T.astype(BF)

    def all_rows(c, first, g):
        for i in range(first, 4):
            rows_part(i, c, g)

    def response_chunks():
        scaled(3)
        for i in range(4):
            all_rows(PC + i, i, 3)
            for w, val in enumerate(keys_part(PC + i, i)):
                for b in range(4):
                    kv[b, 2, i, w] = val[b * T:(b + 1) * T]

    def send_back(d, part, place):
        ty = (y + d) % 4
        return remote(kv.at[ty, part], rbuf.at[d - 1, place], ydev(d))

    def sum_block(b, part, place):
        for w in range(2):
            acc4 = kv[y, part, b, w].astype(F32)
            for d in range(3):
                acc4 = acc4 + rbuf[d, place, b, w].astype(F32)
            kv[y, part, b, w] = acc4.astype(BF)

    def total(part, place):
        lax.fori_loop(0, 4, lambda b, _: (sum_block(b, part, place), 0)[1], 0)

    def join(ty):
        for b in range(4):
            for w in range(2):
                kv[ty, grp, b, w] = (kv[ty, grp, b, w].astype(F32) + zbuf[ty, b, w].astype(F32)).astype(BF)

    hops = (2, 1, 3, 0)
    back_resp = [send_back(d, 2, 0) for d in (2, 1, 3)]
    back_prompt = [send_back(d, grp, 1) for d in (2, 1, 3)]
    crossing = []
    for d in hops:
        ty = (y + d) % 4
        crossing.append(remote(kv.at[ty, half(OTHER)], zbuf.at[ty], xdev(0, 1)))
    kept, asks = [], []
    for e in (2, 1, 3, 0):
        tx = (x + e) % 4
        copy = local if e == 0 else functools.partial(remote, dev=xdev(e))
        asks.append(copy(q_ref.at[tx], query_grad.at[resp, :, wide(kvh)]))
        for w, out in ((0, key_grad), (1, value_grad)):
            kept.append(copy(kv.at[y, 2, tx, w], out.at[resp, :, hd(kvh)]))

    def put(p, ty, part):
        for w, val in enumerate(keys_part(p, 0)):
            for b in range(4):
                kv[ty, part, b, w] = val[b * T:(b + 1) * T]

    spots = [uses.index(((4 - d) % 4, kind)) for kind in (OTHER, OWN) for d in hops]

    def pick(n, table):
        return functools.reduce(lambda v, k: jnp.where(n == k, table[k], v), range(1, len(table)), table[0])

    def prompt_chunk(n, _):
        p = pick(n, spots)
        ty = (y + pick(n, hops * 2)) % 4
        part = half(jnp.where(n < 4, OTHER, OWN))

        @pl.when(n == 1)
        def _():
            response_chunks()
            start(back_resp)

        g = p // 2 + p // 6
        scaled(g)
        for i in range(4):
            rows_part(i, p, g)
        put(p, ty, part)
        for k in range(4):
            @pl.when(n == k)
            def _():
                crossing[k].start()

        for k in range(3):
            @pl.when(n == 4 + k)
            def _():
                crossing[k].wait()
                join(ty)
                back_prompt[k].start()

        @pl.when(n == 5)
        def _():
            wait(back_resp)
            total(2, 0)
            start(kept)

        return 0

    lax.fori_loop(0, 7, prompt_chunk, 0)
    scaled(spots[7] // 2)
    for i in range(4):
        rows_part(i, spots[7], spots[7] // 2)
    for i in range(4):
        for h in range(HEADS):
            rs = slice(h * T, (h + 1) * T)
            q_ref[i, :, rs] = (acc[i, rs, :T] * acc[i, rs, T:]).astype(BF)
    start(asks)
    put(spots[7], y, grp)
    crossing[3].wait()
    join(y)
    wait(back_prompt)
    tail = [remote(kv.at[y, grp, (x + e) % 4], pbuf.at[x], xdev(e)) for e in (2, 1, 3)]
    for e, copy in zip((2, 1, 3), tail):
        sum_block((x + e) % 4, grp, 1)
        copy.start()
    sum_block(x, grp, 1)
    pbuf[x] = kv[y, grp, x]
    wait(tail)
    for j in range(2):
        for w, out in ((0, pk_grad), (1, pv_grad)):
            out[:, j * T:(j + 1) * T] = (pbuf[j, w].astype(F32) + pbuf[2 + j, w].astype(F32)).astype(BF)
    wait(homes + kept + asks)
    assert counter[0] <= N_SEM and counter[1] <= N_SEM


def settle(*refs):
    n = len(refs) // 3
    arrived, left = refs[3 * n:]
    loads = [pltpu.make_async_copy(refs[k], refs[2 * n + k], arrived.at[k]) for k in range(n)]
    stores = [pltpu.make_async_copy(refs[2 * n + k], refs[n + k], left.at[k]) for k in range(n)]
    for copy in loads:
        copy.start()
    for load, store in zip(loads, stores):
        load.wait()
        store.start()
    for copy in stores:
        copy.wait()


def shards(queries, keys, values, prefix_keys, shared_prompt_values, lengths, grad_out):
    like = lambda a: jax.ShapeDtypeStruct(a.shape, BF)
    hbm = pl.BlockSpec(memory_space=pl.ANY)
    vmem = pl.BlockSpec(memory_space=pltpu.VMEM)
    V = pltpu.VMEM
    shapes = [like(queries), like(queries), like(keys), like(keys), like(prefix_keys), like(prefix_keys)]
    made = pl.pallas_call(
        kernel,
        out_shape=shapes,
        in_specs=[pl.BlockSpec(memory_space=pltpu.SMEM)] + [hbm] * 6,
        out_specs=[hbm] * 4 + [vmem] * 2,
        scratch_shapes=[
            V((4, T, R), BF), V((4, T, R), BF), V((4, 3, 4, 2, T, T), BF), V((3, 2, 4, 2, T, T), BF),
            V((4, 4, 2, T, T), BF), V((4, 2, T, T), BF),
            V((6144, 256), BF), V((6144, 256), BF), V((4, R, 256), BF),
            V((2, 4, T, R), BF), V((2, T, 4 * R), BF), V((4, R, CH), F32), V((4, R, CH), BF), V((42, R, CH), BF),
            V((4, R, T), F32), V((4, R, T), F32), V((4, 8, R), F32), V((4, R, 256), F32),
            pltpu.SemaphoreType.DMA((N_SEM,)), pltpu.SemaphoreType.DMA((N_SEM,)),
            pltpu.SemaphoreType.DMA((N_SEM,)),
        ],
        compiler_params=pltpu.CompilerParams(
            collective_id=0, has_side_effects=True, vmem_limit_bytes=64 * 1024 * 1024
        ),
        name="attention",
    )(lengths, queries, keys, values, prefix_keys, shared_prompt_values, grad_out)
    return pl.pallas_call(
        settle,
        out_shape=shapes,
        in_specs=[hbm] * 6,
        out_specs=[hbm] * 6,
        scratch_shapes=[V(a.shape, BF) for a in shapes] + [pltpu.SemaphoreType.DMA((6,))] * 2,
        name="settle",
    )(*made)


def solution(mesh):
    acts, prompt = P("grp", "ctx", "head"), P(("grp", "ctx"), "head")
    return jax.shard_map(
        shards,
        mesh=mesh,
        in_specs=(acts, acts, acts, prompt, prompt, P("grp"), acts),
        out_specs=(acts, acts, acts, acts, prompt, prompt),
        check_vma=False,
    )
```

```python
import functools
import math

import jax
import jax.numpy as jnp
from jax import lax
from jax.experimental import pallas as pl
from jax.experimental.pallas import tpu as pltpu
from jax.sharding import PartitionSpec as P

MESH = pl.DeviceIdType.MESH
F32, BF = jnp.float32, jnp.bfloat16
T = 128
CH = 512
HEADS = 5
R = HEADS * T
PC = 8
NT = (((1,), (1,)), ((), ()))
NN = (((1,), (0,)), ((), ()))
dot = functools.partial(lax.dot_general, preferred_element_type=F32)
N_SEM = 64


def mult(v, n):
    return pl.multiple_of(v, n)


def kernel(
    lens_ref, queries, keys, values, pkeys, pvalues, gout,
    attended, query_grad, key_grad, value_grad, pk_grad, pv_grad,
    q_ref, g_ref, kv, rbuf, zbuf, pbuf,
    ka, va, qa, gt, gs, s_ref, ds_ref, e_ref, mrun, stat, turned, acc,
    send, recv, lsem,
):
    grp, ctx, head = lax.axis_index("grp"), lax.axis_index("ctx"), lax.axis_index("head")
    x, y = ctx // 4, ctx % 4
    resp, kvh = x // 2, x % 2
    c2 = 1.4426950408889634 / math.sqrt(T)
    scale = 1.0 / math.sqrt(T)

    def xdev(d, other=0):
        return ((grp + other) % 2, ((x + d) % 4) * 4 + y, head)

    def ydev(d):
        return (grp, x * 4 + (y + d) % 4, head)

    counter = [0, 0]

    def remote(src, dst, dev):
        k = counter[0]
        counter[0] += 1
        return pltpu.make_async_remote_copy(
            src_ref=src, dst_ref=dst, send_sem=send.at[k], recv_sem=recv.at[k],
            device_id=dev, device_id_type=MESH,
        )

    def local(src, dst):
        k = counter[1]
        counter[1] += 1
        return pltpu.make_async_copy(src, dst, lsem.at[k])

    partners = [xdev(d) for d in (1, 2, 3)] + [ydev(d) for d in (1, 2, 3)] + [xdev(0, 1)]
    barrier = pltpu.get_barrier_semaphore()
    for dev in partners:
        pl.semaphore_signal(barrier, inc=1, device_id=dev, device_id_type=MESH)
    pl.semaphore_wait(barrier, len(partners))

    def hd(j):
        return pl.ds(mult(j * T, T), T)

    def wide(j):
        return pl.ds(mult(j * R, T), R)

    prompt, mine, asked, given, graded = [], [], [], [], []
    for d in (0, 2, 1, 3):
        tx = (x + d) % 4
        r, j = tx // 2, tx % 2
        copy = local if d == 0 else functools.partial(remote, dev=xdev(d))
        for which, ref in ((0, pkeys), (1, pvalues)):
            prompt.append(copy(ref.at[:, hd(j)], kv.at[y, grp, x, which]))
        (asked if d else mine).append(copy(queries.at[r, :, wide(j)], q_ref.at[x]))
        for which, ref in ((0, keys), (1, values)):
            given.append(copy(ref.at[r, :, hd(j)], kv.at[y, 2, x, which]))
        (graded if d else mine).append(copy(gout.at[r, :, wide(j)], g_ref.at[x]))

    up, down = (y + 1) % 4, (y + 3) % 4

    def near(part):
        return [remote(kv.at[y, part], kv.at[y, part], ydev(d)) for d in (1, 3)]

    def far(part):
        low, high = pl.ds(0, 2), pl.ds(2, 2)
        return [
            remote(kv.at[up, part, low], kv.at[up, part, low], ydev(3)),
            remote(kv.at[down, part, high], kv.at[down, part, high], ydev(1)),
        ]

    def across(d):
        sy = (y - d) % 4
        return [remote(kv.at[sy, grp], kv.at[sy, grp], xdev(0, 1))]

    near_prompt, near_resp, far_prompt, far_resp = near(grp), near(2), far(grp), far(2)
    swap = {d: across(d) for d in range(4)}

    def start(copies):
        for copy in copies:
            copy.start()

    def wait(copies):
        for copy in copies:
            copy.wait()

    start(prompt + mine)
    wait(prompt)
    start(near_prompt + swap[0] + asked)
    wait(near_prompt)
    start(swap[1] + far_prompt + given)

    OWN, OTHER = 0, 1
    uses = [(0, OWN), (0, OTHER), (1, OWN), (3, OWN), (1, OTHER), (2, OWN), (3, OTHER), (2, OTHER)]

    def half(kind):
        return (grp + kind) % 2

    def place(p):
        d, kind = uses[p]
        sy = (y - d) % 4
        for b in range(4):
            rs = slice(p * CH + b * T, p * CH + (b + 1) * T)
            ka[rs, :T] = kv[sy, half(kind), b, 0]
            ka[rs, T:] = kv[sy, half(kind), b, 0]
            va[rs, :T] = kv[sy, half(kind), b, 1]
            va[rs, T:] = jnp.ones((T, T), BF)

    def place_response():
        for sy in range(4):
            for i in range(4):
                rs = slice(4096 + i * CH + sy * T, 4096 + i * CH + (sy + 1) * T)
                ka[rs, :T] = kv[sy, 2, i, 0]
                ka[rs, T:] = kv[sy, 2, i, 0]
                va[rs, :T] = kv[sy, 2, i, 1]
                va[rs, T:] = jnp.ones((T, T), BF)

    def slot(c, i):
        n = c - PC
        if isinstance(c, int) and n >= 0:
            return 32 + 4 * n - (n * (n - 1)) // 2 + i - n
        return 4 * c + i

    def chunk_rows(c):
        return slice(c * CH, (c + 1) * CH) if isinstance(c, int) else pl.ds(mult(c * CH, CH), CH)

    def fold(s):
        return functools.reduce(jnp.maximum, [s[:, k * T:(k + 1) * T] for k in range(CH // T)])

    lane = lax.broadcasted_iota(jnp.int32, (R, T), 1)

    def prepare(i, _):
        for h in range(HEADS):
            rs = slice(h * T, (h + 1) * T)
            qs = q_ref[i, :, rs].astype(F32) * c2
            hi = qs.astype(BF)
            qa[i, rs, :T] = hi
            qa[i, rs, T:] = (qs - hi.astype(F32)).astype(BF)
        return 0

    def clear(i, _):
        acc[i] = jnp.zeros((R, 2 * T), F32)
        mrun[i] = jnp.full((R, T), -jnp.inf, F32)
        stat[i] = jnp.zeros((R, T), F32)
        return 0

    def scores(i, c, slot):
        s = dot(qa[i], ka[chunk_rows(c), :], NT)
        s_ref[slot] = s
        return fold(s)

    def weigh(i, chunks, g, top):
        old = mrun[i]
        new = jnp.maximum(old, jnp.broadcast_to(jnp.max(top, 1, keepdims=True), (R, T)))
        mrun[i] = new
        stat[i] = jnp.where(lane == g, new, stat[i])
        fade = jnp.exp2(old - new)
        es = []
        for c, buf in chunks:
            s = s_ref[buf]
            e = jnp.concatenate(
                [jnp.exp2(s[:, k * T:(k + 1) * T] - new) for k in range(CH // T)], 1
            ).astype(BF)
            e_ref[slot(c, i)] = e
            es.append(e)
        first = chunks[0][0] * CH
        keys_in = pl.ds(first if isinstance(first, int) else mult(first, CH), CH * len(chunks))
        acc[i] = acc[i] * jnp.concatenate([fade, fade], 1) + dot(jnp.concatenate(es, 1), va[keys_in, :], NN)

    def prefix_group(g):
        for i in range(4):
            chunks = [(2 * g + n, (i % 2) * 2 + n) for n in range(2)]
            top = functools.reduce(jnp.maximum, [scores(i, c, buf) for c, buf in chunks])
            weigh(i, chunks, g + g // 3, top)

    def response_tile(i):
        tops = [scores(i, PC + n, n) for n in range(i)]
        s = dot(qa[i], ka[chunk_rows(PC + i), :], NT)
        col = lax.broadcasted_iota(jnp.int32, (T, CH), 1)
        row = lax.broadcasted_iota(jnp.int32, (T, CH), 0) + y * T
        seen = col <= row
        s = jnp.concatenate(
            [jnp.where(seen, s[h * T:(h + 1) * T], -jnp.inf) for h in range(HEADS)], 0
        )
        s_ref[i] = s
        tops.append(fold(s))
        weigh(i, [(PC + n, n) for n in range(i + 1)], 3, functools.reduce(jnp.maximum, tops))

    def conclude(i):
        stat[i] = jnp.exp2(stat[i] - mrun[i])
        pos = lax.broadcasted_iota(jnp.int32, (T, T), 0) + (i * CH + y * T)
        live = pos < lens_ref[resp]
        part = lax.broadcasted_iota(jnp.int32, (T, T), 1)
        for h in range(HEADS):
            rs = slice(h * T, (h + 1) * T)
            inv = 1.0 / acc[i, rs, T:]
            o = jnp.where(live, acc[i, rs, :T] * inv, 0.0).astype(BF)
            g = jnp.where(live, g_ref[i, :, rs].astype(F32), 0.0)
            g_ref[i, :, rs] = o
            d0 = -jnp.sum(g * o.astype(F32), 1, keepdims=True)
            d1 = d0.astype(BF).astype(F32)
            d2 = (d0 - d1).astype(BF).astype(F32)
            d3 = d0 - d1 - d2
            qa[i, rs, :T] = g.astype(BF)
            qa[i, rs, T:] = jnp.where(
                part == 0, d1, jnp.where(part == 1, d2, jnp.where(part == 2, d3, 0.0))
            ).astype(BF)
            gt[0, i, :, rs] = (q_ref[i, :, rs].astype(F32) * (inv * scale)).astype(BF).T
            gt[1, i, :, rs] = (g * inv).astype(BF).T
            turned[i, :, rs] = stat[i, rs, :].T[:8]
            acc[i, rs, T:] = inv * scale
        acc[i, :, :T] = jnp.zeros((R, T), F32)

    lax.fori_loop(0, 4, clear, 0)
    wait(mine + asked)
    lax.fori_loop(0, 4, prepare, 0)

    def group(g, _):
        @pl.when(g == 0)
        def _():
            wait(swap[0])
            start(swap[3])
            place(0)
            place(1)

        @pl.when(g == 1)
        def _():
            wait(given)
            start(near_resp + graded)
            wait(far_prompt)
            start(swap[2])
            place(2)
            place(3)

        @pl.when(g == 2)
        def _():
            wait(near_resp)
            start(far_resp)
            wait(swap[1])
            place(4)
            place(5)

        @pl.when(g == 3)
        def _():
            wait(far_resp)
            place_response()
            for i in range(4):
                response_tile(i)
            wait(swap[3] + swap[2])
            place(6)
            place(7)

        prefix_group(g)
        return 0

    lax.fori_loop(0, 4, group, 0)
    wait(graded)
    for i in range(4):
        conclude(i)

    homes = []
    for d in range(4):
        tx = (x + d) % 4
        copy = local if d == 0 else functools.partial(remote, dev=xdev(d))
        homes.append(copy(g_ref.at[tx], attended.at[resp, :, wide(kvh)]))
    for copy in homes:
        copy.start()

    def scaled(g):
        for i in range(4):
            f = turned[i, pl.ds(g, 1), :]
            for w in range(2):
                gs[w, :, i * R:(i + 1) * R] = (gt[w, i].astype(F32) * f).astype(BF)

    def rows_part(i, c, g):
        kk = chunk_rows(c)
        dp = dot(qa[i], va[kk, :], NT)
        ds = (e_ref[slot(c, i)].astype(F32) * dp).astype(BF)
        ds_ref[i] = ds
        f = jnp.sum(jnp.where(lane == g, stat[i], 0.0), 1, keepdims=True)
        acc[i, :, :T] += f * dot(ds, ka[kk, :T], NN)

    def keys_part(c, first):
        n = (4 - first) * R
        base = slot(c, first)
        ds = ds_ref[first:].reshape(n, CH)
        e = e_ref[pl.ds(base, 4 - first)].reshape(n, CH)
        dk = dot(gs[0, :, first * R:], ds, NN)
        dv = dot(gs[1, :, first * R:], e, NN)
        return dk.T.astype(BF), dv.T.astype(BF)

    def all_rows(c, first, g):
        for i in range(first, 4):
            rows_part(i, c, g)

    def response_chunks():
        scaled(3)
        for i in range(4):
            all_rows(PC + i, i, 3)
            for w, val in enumerate(keys_part(PC + i, i)):
                for b in range(4):
                    kv[b, 2, i, w] = val[b * T:(b + 1) * T]

    def send_back(d, part, place):
        ty = (y + d) % 4
        return remote(kv.at[ty, part], rbuf.at[d - 1, place], ydev(d))

    def sum_block(b, part, place):
        for w in range(2):
            acc4 = kv[y, part, b, w].astype(F32)
            for d in range(3):
                acc4 = acc4 + rbuf[d, place, b, w].astype(F32)
            kv[y, part, b, w] = acc4.astype(BF)

    def total(part, place):
        lax.fori_loop(0, 4, lambda b, _: (sum_block(b, part, place), 0)[1], 0)

    def join(ty):
        for b in range(4):
            for w in range(2):
                kv[ty, grp, b, w] = (kv[ty, grp, b, w].astype(F32) + zbuf[ty, b, w].astype(F32)).astype(BF)

    hops = (2, 1, 3, 0)
    back_resp = [send_back(d, 2, 0) for d in (2, 1, 3)]
    back_prompt = [send_back(d, grp, 1) for d in (2, 1, 3)]
    crossing = []
    for d in hops:
        ty = (y + d) % 4
        crossing.append(remote(kv.at[ty, half(OTHER)], zbuf.at[ty], xdev(0, 1)))
    kept, asks = [], []
    for e in (2, 1, 3, 0):
        tx = (x + e) % 4
        copy = local if e == 0 else functools.partial(remote, dev=xdev(e))
        asks.append(copy(q_ref.at[tx], query_grad.at[resp, :, wide(kvh)]))
        for w, out in ((0, key_grad), (1, value_grad)):
            kept.append(copy(kv.at[y, 2, tx, w], out.at[resp, :, hd(kvh)]))

    def put(p, ty, part):
        for w, val in enumerate(keys_part(p, 0)):
            for b in range(4):
                kv[ty, part, b, w] = val[b * T:(b + 1) * T]

    spots = [uses.index(((4 - d) % 4, kind)) for kind in (OTHER, OWN) for d in hops]

    def pick(n, table):
        return functools.reduce(lambda v, k: jnp.where(n == k, table[k], v), range(1, len(table)), table[0])

    def prompt_chunk(n, _):
        p = pick(n, spots)
        ty = (y + pick(n, hops * 2)) % 4
        part = half(jnp.where(n < 4, OTHER, OWN))

        @pl.when(n == 1)
        def _():
            response_chunks()
            start(back_resp)

        g = p // 2 + p // 6
        scaled(g)
        for i in range(4):
            rows_part(i, p, g)
        put(p, ty, part)
        for k in range(4):
            @pl.when(n == k)
            def _():
                crossing[k].start()

        for k in range(3):
            @pl.when(n == 4 + k)
            def _():
                crossing[k].wait()
                join(ty)
                back_prompt[k].start()

        @pl.when(n == 5)
        def _():
            wait(back_resp)
            total(2, 0)
            start(kept)

        return 0

    lax.fori_loop(0, 7, prompt_chunk, 0)
    scaled(spots[7] // 2)
    for i in range(4):
        rows_part(i, spots[7], spots[7] // 2)
    for i in range(4):
        for h in range(HEADS):
            rs = slice(h * T, (h + 1) * T)
            q_ref[i, :, rs] = (acc[i, rs, :T] * acc[i, rs, T:]).astype(BF)
    start(asks)
    put(spots[7], y, grp)
    crossing[3].wait()
    join(y)
    wait(back_prompt)
    tail = [remote(kv.at[y, grp, (x + e) % 4], pbuf.at[x], xdev(e)) for e in (2, 1, 3)]
    for e, copy in zip((2, 1, 3), tail):
        sum_block((x + e) % 4, grp, 1)
        copy.start()
    sum_block(x, grp, 1)
    pbuf[x] = kv[y, grp, x]
    wait(tail)
    for j in range(2):
        for w, out in ((0, pk_grad), (1, pv_grad)):
            out[:, j * T:(j + 1) * T] = (pbuf[j, w].astype(F32) + pbuf[2 + j, w].astype(F32)).astype(BF)
    wait(homes + kept + asks)
    assert counter[0] <= N_SEM and counter[1] <= N_SEM


def settle(*refs):
    n = len(refs) // 3
    arrived, left = refs[3 * n:]
    loads = [pltpu.make_async_copy(refs[k], refs[2 * n + k], arrived.at[k]) for k in range(n)]
    stores = [pltpu.make_async_copy(refs[2 * n + k], refs[n + k], left.at[k]) for k in range(n)]
    for copy in loads:
        copy.start()
    for load, store in zip(loads, stores):
        load.wait()
        store.start()
    for copy in stores:
        copy.wait()


def shards(queries, keys, values, prefix_keys, shared_prompt_values, lengths, grad_out):
    like = lambda a: jax.ShapeDtypeStruct(a.shape, BF)
    hbm = pl.BlockSpec(memory_space=pl.ANY)
    vmem = pl.BlockSpec(memory_space=pltpu.VMEM)
    V = pltpu.VMEM
    shapes = [like(queries), like(queries), like(keys), like(keys), like(prefix_keys), like(prefix_keys)]
    made = pl.pallas_call(
        kernel,
        out_shape=shapes,
        in_specs=[pl.BlockSpec(memory_space=pltpu.SMEM)] + [hbm] * 6,
        out_specs=[hbm] * 4 + [vmem] * 2,
        scratch_shapes=[
            V((4, T, R), BF), V((4, T, R), BF), V((4, 3, 4, 2, T, T), BF), V((3, 2, 4, 2, T, T), BF),
            V((4, 4, 2, T, T), BF), V((4, 2, T, T), BF),
            V((6144, 256), BF), V((6144, 256), BF), V((4, R, 256), BF),
            V((2, 4, T, R), BF), V((2, T, 4 * R), BF), V((4, R, CH), F32), V((4, R, CH), BF), V((42, R, CH), BF),
            V((4, R, T), F32), V((4, R, T), F32), V((4, 8, R), F32), V((4, R, 256), F32),
            pltpu.SemaphoreType.DMA((N_SEM,)), pltpu.SemaphoreType.DMA((N_SEM,)),
            pltpu.SemaphoreType.DMA((N_SEM,)),
        ],
        compiler_params=pltpu.CompilerParams(
            collective_id=0, has_side_effects=True, vmem_limit_bytes=64 * 1024 * 1024
        ),
        name="attention",
    )(lengths, queries, keys, values, prefix_keys, shared_prompt_values, grad_out)
    return pl.pallas_call(
        settle,
        out_shape=shapes,
        in_specs=[hbm] * 6,
        out_specs=[hbm] * 6,
        scratch_shapes=[V(a.shape, BF) for a in shapes] + [pltpu.SemaphoreType.DMA((6,))] * 2,
        name="settle",
    )(*made)


def solution(mesh):
    acts, prompt = P("grp", "ctx", "head"), P(("grp", "ctx"), "head")
    return jax.shard_map(
        shards,
        mesh=mesh,
        in_specs=(acts, acts, acts, prompt, prompt, P("grp"), acts),
        out_specs=(acts, acts, acts, acts, prompt, prompt),
        check_vma=False,
    )
```
